256 devices in a mesh: ctx: 32 (over y, z), head: 8 (over x, core).
Axes of the slice: x: 4, y: 4, z: 8, core: 2. Of those that a mesh axis runs over, the one named last changes fastest.
Arguments:
- queries: bfloat16 [32768, 128], P('ctx'), may hold values from -2 to 2
- keys: bfloat16 [32768, 128], P('ctx'), may hold values from -2 to 2
- values: bfloat16 [32768, 2048], P('ctx', 'head'), may hold values from -6 to 6
- gates: float32 [16, 32768], P('head', 'ctx'), may hold values from -2.5 to 0
- level_weights: float32 [16, 10, 32768], P('head', None, 'ctx'), may hold values from 0 to 4
- segment: int32 [32768], P('ctx'), may hold values from 0 to 7, never falling along the last dimension, each value on 1 to 16384 neighbouring positions
- cotangent: bfloat16 [32768, 2048], P('ctx', 'head'), may hold values from -0.59765625 to 0.59765625
Outputs:
- query_grad: float32 [32768, 128], P(('ctx', 'head'))
- key_grad: float32 [32768, 128], P(('ctx', 'head'))
- value_grad: float32 [32768, 2048], P('ctx', 'head')
- gate_grad: float32 [16, 32768], P('head', 'ctx')
- weight_grad: float32 [16, 10, 32768], P('head', None, 'ctx')
The draws below stay inside these ranges and needn't reach their ends.
Inputs may be any that keep to these rules, and one draw needn't show every extreme that they name: `segment`: document numbers never fall along the tokens; every number is used, each document holds 1 to 16384 tokens and one holds exactly that many.
All inputs are finite; a program needn't handle non-finite values.
Results may differ from the reference program's by a relative error of at most 0.0003.
Values sent between devices are 32-bit elements; how exact they have to be, the bound alone decides.
A program may use at most 64 MiB of HBM per device.

```python
import math
import jax
import jax.numpy as jnp
import numpy as np
from jax import lax

HEAD_COUNT = 16
DS = 128
DV = 128
STRETCH = 128
LEVELS = 10
TOK_DEV = 1024
TOKEN_COUNT = 32768
N_CTX = 32


def draw_gates(key, part):
    random_subkeys = jax.random.split(key, 6)
    head_order = jax.random.permutation(random_subkeys[0], HEAD_COUNT)
    slow_heads = head_order < HEAD_COUNT // 2
    mixing = jax.random.uniform(random_subkeys[1], (HEAD_COUNT,), jnp.float32)
    slow_rate = jnp.exp(jnp.log(0.1 / TOKEN_COUNT) + mixing * jnp.log(6.0))
    fast_rate = jnp.exp(jnp.log(1.0 / 2000.0) + mixing * jnp.log(2000.0 / 30.0))
    baseline_rate = jnp.where(slow_heads, slow_rate, fast_rate)
    shard_scale = jnp.exp(jax.random.uniform(random_subkeys[2], (HEAD_COUNT, TOKEN_COUNT // TOK_DEV), jnp.float32, -0.7, 0.7))
    shard_scale = jnp.repeat(shard_scale, TOK_DEV, axis=1)
    entry_scale = jnp.exp(jax.random.uniform(random_subkeys[3], (HEAD_COUNT, TOKEN_COUNT), jnp.float32, -0.7, 0.7))
    spike_position = jax.random.randint(random_subkeys[4], (HEAD_COUNT, 3), 0, TOKEN_COUNT)
    spike_loss = jax.random.uniform(random_subkeys[5], (HEAD_COUNT, 3), jnp.float32, 0.2, 0.5)
    spike_hits = jnp.arange(TOKEN_COUNT)[None, None, :] == spike_position[:, :, None]
    spike_events = jnp.sum(jnp.where(spike_hits, jnp.log(1.0 - spike_loss)[:, :, None], 0.0), axis=1)
    return -(baseline_rate[:, None] * shard_scale * entry_scale) + spike_events


def draw_level_weights(key, part):
    level_idx = jnp.arange(LEVELS)
    bucket_size = jnp.where(level_idx == 0, STRETCH / 2.0, STRETCH * 2.0 ** jnp.maximum(level_idx - 1, 0))
    base_weight = bucket_size.astype(jnp.float32) ** (-0.5)
    spread = jnp.exp(jax.random.uniform(key, (HEAD_COUNT, LEVELS, TOKEN_COUNT), jnp.float32, -0.7, 0.7))
    return base_weight[None, :, None] * spread


def levels(own_key, extent, cuts, low, top_value):
    factor_of, own = 1.0, jax.random.fold_in(own_key, 6)
    for dim, blocks in cuts:
        draws = jnp.exp(jax.random.uniform(jax.random.fold_in(own, dim), (blocks,), jnp.float32, low / len(cuts), top_value / len(cuts)))
        factor_of = factor_of * jnp.repeat(draws, extent[dim] // blocks).reshape([-1 if axis == dim else 1 for axis in range(len(extent))])
    return factor_of


def profile(number_of, total, bound, lean):
    weights = [(1 << 20) // math.isqrt(rank ** lean) + 1 for rank in range(2, number_of + 1)]
    spare, holding = total - bound - (number_of - 1), [1] * (number_of - 1)
    while spare > 0:
        free = [i for i in range(number_of - 1) if holding[i] < bound]
        whole, left = sum([weights[i] for i in free]), spare
        for i in free:
            extra = min(bound - holding[i], max(1, left * weights[i] // whole), spare)
            holding[i] = holding[i] + extra
            spare = spare - extra
    return np.array([bound] + holding)


def ragged_sizes(stream_key, count, total, limit, skew):
    if count == 2:
        one = jax.random.randint(stream_key, (), max(1, total - limit), min(limit, total - 1) + 1)
        return jnp.stack([one, total - one])
    sizes = jnp.asarray(profile(count, total, limit, skew), jnp.int32)
    pairs = (count - 1) // 2
    source_of, sink = sizes[1:1 + 2 * pairs:2], sizes[2:2 + 2 * pairs:2]
    slack = jnp.minimum(source_of - 1, limit - sink)
    shifted = jax.random.randint(jax.random.fold_in(stream_key, 1), (pairs,), 0, 1 << 20) % (slack + 1)
    sizes = sizes.at[1:1 + 2 * pairs:2].set(source_of - shifted).at[2:2 + 2 * pairs:2].set(sink + shifted)
    return sizes[jax.random.permutation(jax.random.fold_in(stream_key, 2), count)]


def noise(stream_key, shape, width, bound, pieces=(), kind=jnp.bfloat16):
    loudness = levels(stream_key, shape, pieces, -0.22, 0.18) if pieces else 1.0
    result = jax.random.normal(stream_key, shape, jnp.float32) * width * loudness
    return jnp.minimum(jnp.maximum(result, -bound), bound).astype(kind)


def setup_inputs(seed: int = 0) -> dict:
    splits = jax.random.split(jax.random.key(seed), 8)
    return {
        "queries": noise(splits[0], (TOKEN_COUNT, DS), 0.3, 2.0, ((0, 32),)),
        "keys": noise(splits[1], (TOKEN_COUNT, DS), 0.3, 2.0, ((0, 32),)),
        "values": noise(splits[2], (TOKEN_COUNT, HEAD_COUNT * DV), 1.0, 6.0, ((0, 32), (1, 8))),
        "gates": draw_gates(jax.random.fold_in(splits[7], 71), 0),
        "level_weights": draw_level_weights(jax.random.fold_in(splits[7], 71), 0),
        "segment": jnp.searchsorted(jnp.cumsum(ragged_sizes(splits[5], N_CTX // 4, TOKEN_COUNT, TOKEN_COUNT // 2, 0)), jnp.arange(TOKEN_COUNT), side="right").astype(jnp.int32),
        "cotangent": noise(splits[6], (TOKEN_COUNT, HEAD_COUNT * DV), 0.09, 0.59765625, ((0, 32), (1, 8))),
    }


PRECISE = lax.Precision.HIGHEST

def stretch_tables(gates, segment):
    num_stretches = segment.shape[0] // STRETCH
    seg_stretches = segment.reshape(num_stretches, STRETCH)
    within = jnp.cumsum(gates.reshape(num_stretches, STRETCH), axis=1)
    stretch_total = within[:, -1]
    return (seg_stretches, within, stretch_total, jnp.cumsum(stretch_total), seg_stretches[:, -1])

def stretch_mix(query_stretches, key_stretches, value_stretches, seg_stretches, within, first_weight):
    offsets = jnp.arange(STRETCH)
    causal = offsets[:, None] >= offsets[None, :]
    allowed = causal[None] & (seg_stretches[:, :, None] == seg_stretches[:, None, :])
    decays = jnp.where(allowed, jnp.exp(jnp.minimum(within[:, :, None] - within[:, None, :], 0.0)), 0.0)
    scores = jnp.einsum('cti,csi->cts', query_stretches, key_stretches, precision=PRECISE)
    return jnp.einsum('cts,csj->ctj', first_weight[:, :, None] * decays * scores, value_stretches, precision=PRECISE)

def merge_blocks(blocks, block_span, stretch_cum, seg_end):
    num_blocks = blocks.shape[0]
    block_ends = jnp.arange(num_blocks) * block_span + block_span - 1
    lower_end = block_ends[0::2]
    upper_end = block_ends[1::2]
    linkage = jnp.where(seg_end[lower_end] == seg_end[upper_end], jnp.exp(jnp.minimum(stretch_cum[upper_end] - stretch_cum[lower_end], 0.0)), 0.0)
    return blocks[0::2] * linkage[:, None, None] + blocks[1::2]

def bridge(source_end, active, prior_stretch, stretch_cum, seg_end):
    source = jnp.maximum(source_end, 0)
    allowed = active & (seg_end[source] == seg_end[prior_stretch])
    return jnp.where(allowed, jnp.exp(jnp.minimum(stretch_cum[prior_stretch] - stretch_cum[source], 0.0)), 0.0)

def half_level(queries, blocks, block_span, token_weight):
    num_stretches = token_weight.shape[0]
    num_pairs = num_stretches // (2 * block_span)
    paired_weight = token_weight.reshape(num_pairs, 2, block_span * STRETCH)
    query_pairs = queries.reshape(num_pairs, 2, block_span * STRETCH, queries.shape[1])
    upper_out = jnp.einsum('nti,nij->ntj', query_pairs[:, 1] * paired_weight[:, 1, :, None], blocks[0::2], precision=PRECISE)
    return jnp.stack([jnp.zeros_like(upper_out), upper_out], axis=1).reshape(num_stretches * STRETCH, upper_out.shape[2])

def head_forward(queries, keys, values, gates, weights, segment):
    length = queries.shape[0]
    num_stretches = length // STRETCH
    seg_stretches, within, stretch_total, stretch_cum, seg_end = stretch_tables(gates, segment)
    weight_stretches = weights.reshape(LEVELS, num_stretches, STRETCH)
    key_stretches = keys.reshape(num_stretches, STRETCH, -1)
    value_stretches = values.reshape(num_stretches, STRETCH, -1)
    summed = stretch_mix(queries.reshape(num_stretches, STRETCH, -1), key_stretches, value_stretches, seg_stretches, within, weight_stretches[0]).reshape(length, -1)
    key_weight = jnp.where(seg_stretches == seg_end[:, None], jnp.exp(stretch_total[:, None] - within), 0.0)
    blocks = jnp.einsum('csi,csj->cij', key_stretches * key_weight[:, :, None], value_stretches, precision=PRECISE)
    prior_end = jnp.concatenate([jnp.full((1,), -1, jnp.int32), seg_end[:-1]])
    query_weight = jnp.where(seg_stretches == prior_end[:, None], jnp.exp(within), 0.0)
    stretch_idx = jnp.arange(num_stretches)
    prior_stretch = jnp.maximum(stretch_idx - 1, 0)
    block_span = 1
    for level_idx in range(1, LEVELS - 1):
        if 2 * block_span <= num_stretches:
            active = stretch_idx // block_span % 2 == 1
            linkage = bridge(stretch_idx // block_span * block_span - 1, active, prior_stretch, stretch_cum, seg_end)
            summed = summed + half_level(queries, blocks, block_span, linkage[:, None] * query_weight * weight_stretches[level_idx])
            blocks = merge_blocks(blocks, block_span, stretch_cum, seg_end)
            block_span = 2 * block_span
    if 2 * block_span <= num_stretches:
        num_blocks = num_stretches // block_span
        block_idx = jnp.arange(num_blocks)
        block_ends = block_idx * block_span + block_span - 1
        before_end = jnp.maximum(block_idx - 1, 0) * block_span + block_span - 1
        allowed = (block_idx[None, :] < block_idx[:, None]) & (seg_end[block_ends][None, :] == seg_end[before_end][:, None])
        prefix_mix = jnp.where(allowed, jnp.exp(jnp.minimum(stretch_cum[before_end][:, None] - stretch_cum[block_ends][None, :], 0.0)), 0.0)
        prefix = jnp.einsum('ab,bij->aij', prefix_mix, blocks, precision=PRECISE)
        linkage = bridge(stretch_idx // block_span * block_span - 1, stretch_idx >= block_span, prior_stretch, stretch_cum, seg_end)
        token_weight = (linkage[:, None] * query_weight * weight_stretches[LEVELS - 1]).reshape(num_blocks, block_span * STRETCH)
        grouped = queries.reshape(num_blocks, block_span * STRETCH, queries.shape[1]) * token_weight[:, :, None]
        summed = summed + jnp.einsum('nti,nij->ntj', grouped, prefix, precision=PRECISE).reshape(length, -1)
    return summed

def reference(queries, keys, values, gates, level_weights, segment, cotangent):
    length = queries.shape[0]
    query_full = queries.astype(jnp.float32)
    key_full = keys.astype(jnp.float32)
    value_heads = values.astype(jnp.float32).reshape(length, HEAD_COUNT, DV).transpose(1, 0, 2)
    cotan_heads = cotangent.astype(jnp.float32).reshape(length, HEAD_COUNT, DV).transpose(1, 0, 2)

    def one_head(carried, head_item):
        value_one, gate_one, weight_one, cotan_one = head_item

        def forward(query_in, key_in, value_in, gate_in, weight_in):
            return head_forward(query_in, key_in, value_in, gate_in, weight_in, segment)
        _, pullback = jax.vjp(forward, query_full, key_full, value_one, gate_one, weight_one)
        query_part, key_part, value_part, gate_part, weight_part = pullback(cotan_one)
        return ((carried[0] + query_part, carried[1] + key_part), (value_part, gate_part, weight_part))
    initial = (jnp.zeros((length, DS), jnp.float32), jnp.zeros((length, DS), jnp.float32))
    (query_grad, key_grad), (value_parts, gate_grad, weight_grad) = lax.scan(one_head, initial, (value_heads, gates, level_weights, cotan_heads))
    value_grad = value_parts.transpose(1, 0, 2).reshape(length, HEAD_COUNT * DV)
    return (query_grad, key_grad, value_grad, gate_grad, weight_grad)
```

```python
import functools

import jax
import jax.numpy as jnp
from jax import lax
from jax.experimental import pallas as pl
from jax.experimental.pallas import tpu as pltpu
from jax.sharding import PartitionSpec as P

STRETCH = 128
LOCAL_LEVELS = 3
EXTRA = 2
F32 = jnp.float32
BF16 = jnp.bfloat16


def halves(x):
    high = x.astype(BF16)
    return high, (x - high.astype(F32)).astype(BF16)


def thirds(x):
    high = x.astype(BF16)
    rest = x - high.astype(F32)
    middle = rest.astype(BF16)
    return high, middle, (rest - middle.astype(F32)).astype(BF16)


def dot(a, b):
    return jnp.dot(a, b, preferred_element_type=F32)


def dot_nt(a, b):
    return lax.dot_general(a, b, (((1,), (1,)), ((), ())), preferred_element_type=F32)


def dot_left(x, exact):
    high, low = halves(x)
    return dot(high, exact) + dot(low, exact)


def dot_right(exact, x):
    high, low = halves(x)
    return dot(exact, high) + dot(exact, low)


def sum_of(terms):
    return functools.reduce(jnp.add, terms)


def ones_where(mask):
    return jnp.where(mask, 1.0, 0.0).astype(BF16)


def part(c):
    return slice(c * STRETCH, (c + 1) * STRETCH)


def pop(number, bits):
    return sum_of([(number >> b) & 1 for b in range(bits)])


def kernel(
    n_ctx,
    n_head,
    q_ref,
    k_ref,
    v_ref,
    c_ref,
    g_ref,
    w_ref,
    s_ref,
    dq_ref,
    dk_ref,
    dv_ref,
    dg_ref,
    dw_ref,
    qt_ref,
    kt_ref,
    qtb_ref,
    ktb_ref,
    ctb_ref,
    block_ref,
    out1,
    buf1,
    out2,
    buf2,
    dqt_ref,
    dk_acc,
    head_out,
    head_in,
    sems,
):
    heads, tokens = g_ref.shape
    num = tokens // STRETCH
    rows = heads * num
    bits = n_ctx.bit_length() - 1
    slabs = EXTRA + bits
    slab_rows = buf1.shape[1]
    per_head = n_ctx // heads
    me = lax.axis_index("ctx")
    mine = lax.axis_index("head")
    count = pop(me, bits)
    everything = sum(EXTRA + bin(n).count("1") for n in range(n_ctx))

    barrier = pltpu.get_barrier_semaphore()

    def greet_ctx(k, _):
        pl.semaphore_signal(barrier, inc=1, device_id={"ctx": lax.rem(me + k, n_ctx)})
        return 0

    def greet_head(k, _):
        pl.semaphore_signal(barrier, inc=1, device_id={"head": lax.rem(mine + k, n_head)})
        return 0

    lax.fori_loop(1, n_ctx, greet_ctx, 0)
    lax.fori_loop(1, n_head, greet_head, 0)

    gates = jnp.concatenate(
        [g_ref[h : h + 1, part(c)] for h in range(heads) for c in range(num)], axis=0
    )
    seg_one = s_ref[...]
    seg = jnp.concatenate([seg_one] * heads, axis=0)
    row_at = lax.broadcasted_iota(jnp.int32, (STRETCH, STRETCH), 0)
    lane_at = lax.broadcasted_iota(jnp.int32, (STRETCH, STRETCH), 1)
    upto = ones_where(row_at <= lane_at)
    within = sum_of([dot(x, upto) for x in thirds(gates)])
    total = jnp.broadcast_to(within[:, STRETCH - 1 :], within.shape)
    seg_end = jnp.broadcast_to(seg[:, STRETCH - 1 :], seg.shape)
    seg_first = jnp.broadcast_to(seg_one[:, :1], seg_one.shape)[:1]
    ra = lax.broadcasted_iota(jnp.int32, (rows, rows), 0)
    rb = lax.broadcasted_iota(jnp.int32, (rows, rows), 1)
    same_head = (ra // num) == (rb // num)
    earlier = ones_where(same_head & (rb < ra))
    later = ones_where(same_head & (rb > ra))
    before = sum_of([dot(earlier, x) for x in thirds(total)])
    entry = jnp.where(seg == seg_first, jnp.exp(within + before), 0.0)
    key_weight = jnp.where(seg == seg_end, jnp.exp(total - within), 0.0)
    through_exp = jnp.exp(total)

    def end(c):
        return seg_end[c : c + 1]

    def through(h, c):
        r = h * num + c
        return jnp.where(end(c - 1) == end(c), through_exp[r : r + 1], 0.0)

    def local_weight(h, level, c):
        r = h * num + c
        span = 1 << (level - 1)
        base = c // span * span
        shift = before[r : r + 1] - before[h * num + base : h * num + base + 1]
        return jnp.where(
            seg[r : r + 1] == end(base - 1), jnp.exp(within[r : r + 1] + shift), 0.0
        )

    def remote_row(h, k, c):
        picked = jnp.zeros((1, STRETCH), F32)
        for b in range(bits):
            is_it = (((me >> b) & 1) == 1) & (pop(me & ((1 << b) - 1), bits) == k)
            level = LOCAL_LEVELS + 1 + b
            picked = picked + jnp.where(is_it, w_ref[h, level : level + 1, part(c)], 0.0)
        return picked

    def columns(ref, h):
        return ref[:, h * STRETCH : (h + 1) * STRETCH]

    qt_ref[...] = q_ref[...].astype(F32).T
    kt_ref[...] = k_ref[...].astype(F32).T
    qtb_ref[...] = qt_ref[...].astype(BF16)
    ktb_ref[...] = kt_ref[...].astype(BF16)
    for h in range(heads):
        ctb_ref[h] = columns(c_ref, h).astype(F32).T.astype(BF16)

    for h in range(heads):
        for c in range(num):
            r = h * num + c
            scaled = kt_ref[:, part(c)] * key_weight[r : r + 1]
            block_ref[h, c] = dot_left(scaled, v_ref[part(c), h * STRETCH : (h + 1) * STRETCH])
        state = block_ref[h, 0]
        for c in range(1, num):
            state = through(h, c) * state + block_ref[h, c]
        last = h * num + num - 1
        passes = jnp.where(
            seg_first == end(num - 1), jnp.exp(before[last : last + 1] + total[last : last + 1]), 0.0
        )
        at = lax.broadcasted_iota(jnp.int32, (slab_rows, STRETCH), 0)
        meta = jnp.where(
            at == 0,
            passes,
            jnp.where(at == 1, seg_first.astype(F32), end(num - 1).astype(F32)),
        )
        for i in range(per_head):
            to = (h * per_head + i) * slabs
            out1[to] = meta
            out1[to + 1] = state[i * slab_rows : (i + 1) * slab_rows]

    for k in range(bits):

        @pl.when(count > k)
        def _(k=k):
            for h in range(heads):
                scaled = jnp.concatenate(
                    [
                        qt_ref[:, part(c)]
                        * (entry[h * num + c : h * num + c + 1] * remote_row(h, k, c))
                        for c in range(num)
                    ],
                    axis=1,
                )
                grad = dot_left(scaled, columns(c_ref, h))
                for i in range(per_head):
                    out1[(h * per_head + i) * slabs + EXTRA + k] = grad[
                        i * slab_rows : (i + 1) * slab_rows
                    ]

    pl.semaphore_wait(barrier, n_ctx + n_head - 2)

    for size in range(bits + 1):

        @pl.when(count == size)
        def _(size=size):
            def send(k, _):
                to = lax.rem(me + k, n_ctx)
                pltpu.make_async_remote_copy(
                    src_ref=out1.at[pl.ds(to * slabs, EXTRA + size)],
                    dst_ref=buf1.at[pl.ds(me * slabs, EXTRA + size)],
                    send_sem=sems.at[0],
                    recv_sem=sems.at[1],
                    device_id={"ctx": to},
                ).start()
                return 0

            lax.fori_loop(1, n_ctx, send, 0)
            for s in range(EXTRA + size):
                buf1[me * slabs + s] = out1[me * slabs + s]

    ones = jnp.ones((8, STRETCH), BF16)
    key_terms = [None] * rows
    query_terms = [None] * rows
    for c in range(num):
        seg_row = seg_one[c : c + 1]
        seg_col = jnp.broadcast_to(seg_row.astype(F32), (STRETCH, STRETCH)).T
        allowed = (row_at <= lane_at) & (seg_col == seg_row.astype(F32))
        scores = dot(k_ref[part(c), :], qtb_ref[:, part(c)])
        dk_sum = None
        dq_sum = None
        for h in range(heads):
            r = h * num + c
            cols = slice(h * STRETCH, (h + 1) * STRETCH)
            w_row = within[r : r + 1]
            w_col = jnp.broadcast_to(w_row, (STRETCH, STRETCH)).T
            decay = jnp.where(allowed, jnp.exp(jnp.minimum(w_row - w_col, 0.0)), 0.0)
            pairs = dot(v_ref[part(c), cols], ctb_ref[h, :, part(c)])
            mixed = decay * scores
            weight = w_ref[h, 0:1, part(c)]
            d_weight = jnp.sum(mixed * pairs, axis=0, keepdims=True)
            dw_ref[h, 0:1, part(c)] = d_weight
            query_terms[r] = weight * d_weight
            dv_ref[part(c), cols] = dot_left(mixed * weight, c_ref[part(c), cols])
            d_scores = decay * pairs * weight
            dk_one = dot_left(d_scores, q_ref[part(c), :])
            dq_one = dot_right(ktb_ref[:, part(c)], d_scores)
            products = k_ref[part(c), :].astype(F32) * dk_one
            key_terms[r] = sum_of([dot_nt(ones, x) for x in thirds(products)])[:1]
            dk_sum = dk_one if dk_sum is None else dk_sum + dk_one
            dq_sum = dq_one if dq_sum is None else dq_sum + dq_one
        dk_acc[part(c), :] = dk_sum
        dqt_ref[:, part(c)] = dq_sum

    for size in range(bits + 1):

        @pl.when(count == size)
        def _(size=size):
            got = buf1.at[pl.ds(0, everything - EXTRA - size)]
            pltpu.make_async_copy(got, got, sems.at[1]).wait()

    meta_rows = [[buf1[n * slabs, m : m + 1] for m in range(3)] for n in range(n_ctx)]
    enter = [None] + [
        jnp.where(meta_rows[n - 1][2] == meta_rows[n][1], 1.0, 0.0) for n in range(1, n_ctx)
    ]
    link = [jnp.zeros_like(meta_rows[0][0])] + [
        meta_rows[n][0] * enter[n] for n in range(1, n_ctx)
    ]

    def received(n, s):
        return buf1[n * slabs + s]

    def rank(n, b):
        return bin(n & ((1 << b) - 1)).count("1")

    blocks = [[received(n, 1) for n in range(n_ctx)]]
    passing = [link]
    for b in range(bits):
        low, thru = blocks[b], passing[b]
        half = len(low) // 2
        blocks.append([thru[2 * j + 1] * low[2 * j] + low[2 * j + 1] for j in range(half)])
        passing.append([thru[2 * j] * thru[2 * j + 1] for j in range(half)])
    block_grads = [[None] * (n_ctx >> b) for b in range(bits)]
    flows = [jnp.zeros((slab_rows, STRETCH), F32)] * n_ctx
    for b in range(bits):
        for j in range(1, n_ctx >> b, 2):
            lead = None
            for p in range(j << b, (j + 1) << b):
                lead = jnp.ones((1, STRETCH), F32) if lead is None else lead * link[p - 1]
                factor = lead * enter[p]
                remote = factor * blocks[b][j - 1]
                slot = EXTRA + rank(p, b)
                out2[p * slabs + slot] = remote
                grad = received(p, slot)
                flows[p] = flows[p] + remote * grad
                term = factor * grad
                old = block_grads[b][j - 1]
                block_grads[b][j - 1] = term if old is None else old + term
    down = [jnp.zeros((slab_rows, STRETCH), F32)]
    for b in reversed(range(bits)):
        next_down = []
        for j, top in enumerate(down):
            next_down += [block_grads[b][2 * j] + passing[b][2 * j + 1] * top, top]
        down = next_down
    after = jnp.zeros((slab_rows, STRETCH), F32)
    for n in reversed(range(n_ctx)):
        out2[n * slabs] = down[n]
        out2[n * slabs + 1] = after
        after = after + (flows[n] - received(n, 1) * down[n])

    def send_back(k, _):
        to = lax.rem(me + k, n_ctx)
        size_there = pop(to, bits)
        for size in range(bits + 1):

            @pl.when(size_there == size)
            def _(size=size):
                pltpu.make_async_remote_copy(
                    src_ref=out2.at[pl.ds(to * slabs, EXTRA + size)],
                    dst_ref=buf2.at[pl.ds(me * slabs, EXTRA + size)],
                    send_sem=sems.at[2],
                    recv_sem=sems.at[3],
                    device_id={"ctx": to},
                ).start()

        return 0

    lax.fori_loop(1, n_ctx, send_back, 0)
    for size in range(bits + 1):

        @pl.when(count == size)
        def _(size=size):
            for s in range(EXTRA + size):
                buf2[me * slabs + s] = out2[me * slabs + s]

    state_grads = []
    for h in range(heads):
        cols = slice(h * STRETCH, (h + 1) * STRETCH)
        lower = [block_ref[h, c] for c in range(num)]
        thru = [None] + [through(h, c) for c in range(1, num)]
        thru[0] = jnp.zeros_like(thru[1])
        per_level = []
        thrus = []
        for level in range(1, LOCAL_LEVELS + 1):
            span = 1 << (level - 1)
            grads = [None] * len(lower)
            for j in range(1, len(lower), 2):
                lanes = slice(j * span * STRETCH, (j + 1) * span * STRETCH)
                high, low = halves(lower[j - 1])
                reach = ctb_ref[h, :, lanes]
                got = dot(high, reach) + dot(low, reach)
                scaled = []
                for c in range(j * span, (j + 1) * span):
                    r = h * num + c
                    here = slice((c - j * span) * STRETCH, (c - j * span + 1) * STRETCH)
                    decay = local_weight(h, level, c)
                    q_part = qt_ref[:, part(c)]
                    d_weight = decay * jnp.sum(q_part * got[:, here], axis=0, keepdims=True)
                    weight = w_ref[h, level : level + 1, part(c)]
                    dw_ref[h, level : level + 1, part(c)] = d_weight
                    query_terms[r] = query_terms[r] + weight * d_weight
                    both = weight * decay
                    dqt_ref[:, part(c)] += both * got[:, here]
                    scaled.append(q_part * both)
                scaled = jnp.concatenate(scaled, axis=1) if span > 1 else scaled[0]
                grads[j - 1] = dot_left(scaled, c_ref[lanes, cols])
            for j in range(0, len(lower), 2):
                for c in range(j * span, (j + 1) * span):
                    dw_ref[h, level : level + 1, part(c)] = jnp.zeros((1, STRETCH), F32)
            per_level.append(grads)
            thrus.append(thru)
            lower, thru = (
                [thru[j + 1] * lower[j] + lower[j + 1] for j in range(0, len(lower), 2)],
                [thru[j] * thru[j + 1] for j in range(0, len(lower), 2)],
            )
        down = [None]
        for level in reversed(range(LOCAL_LEVELS)):
            next_down = []
            for j, top in enumerate(down):
                low = per_level[level][2 * j]
                next_down += [low if top is None else low + thrus[level][2 * j + 1] * top, top]
            down = next_down
        for c in range(num - 1):
            block_ref[h, c] = down[c]
        block_ref[h, num - 1] = jnp.zeros((STRETCH, STRETCH), F32)
        state_grads.append(None)

    for size in range(bits + 1):

        @pl.when(count == size)
        def _(size=size):
            got = buf2.at[pl.ds(0, (n_ctx - 1) * (EXTRA + size))]
            pltpu.make_async_copy(got, got, sems.at[3]).wait()

    def gathered(h, s):
        return jnp.concatenate(
            [buf2[(h * per_head + i) * slabs + s] for i in range(per_head)], axis=0
        )

    for h in range(heads):
        cols = slice(h * STRETCH, (h + 1) * STRETCH)
        top = gathered(h, 0)
        for c in reversed(range(num)):
            r = h * num + c
            seg_col = jnp.broadcast_to(seg_one[c : c + 1].astype(F32), (STRETCH, STRETCH)).T
            w_col = jnp.broadcast_to(within[r : r + 1], (STRETCH, STRETCH)).T
            weight = jnp.where(
                seg_col == end(c).astype(F32), jnp.exp(total[r : r + 1] - w_col), 0.0
            )
            high, low = halves(block_ref[h, c] + top)
            keys_here = k_ref[part(c), :]
            values_here = v_ref[part(c), cols]
            dv_ref[part(c), cols] += weight * (dot(keys_here, high) + dot(keys_here, low))
            dk_one = weight * (dot_nt(values_here, high) + dot_nt(values_here, low))
            dk_acc[part(c), :] += dk_one
            products = keys_here.astype(F32) * dk_one
            key_terms[r] = (
                key_terms[r] + sum_of([dot_nt(ones, x) for x in thirds(products)])[:1]
            )
            if c:
                top = through(h, c) * top

    for h in range(heads):
        dw_ref[h, LOCAL_LEVELS + 1 :, :] = jnp.zeros(
            (dw_ref.shape[1] - LOCAL_LEVELS - 1, tokens), F32
        )
    for k in range(bits):

        @pl.when(count > k)
        def _(k=k):
            for h in range(heads):
                high, low = halves(gathered(h, EXTRA + k))
                for c in range(num):
                    reach = ctb_ref[h, :, part(c)]
                    got = dot(high, reach) + dot(low, reach)
                    decay = entry[h * num + c : h * num + c + 1]
                    d_weight = decay * jnp.sum(qt_ref[:, part(c)] * got, axis=0, keepdims=True)
                    dqt_ref[:, part(c)] += (decay * remote_row(h, k, c)) * got
                    for b in range(bits):
                        is_it = (((me >> b) & 1) == 1) & (pop(me & ((1 << b) - 1), bits) == k)
                        level = LOCAL_LEVELS + 1 + b
                        dw_ref[h, level : level + 1, part(c)] += jnp.where(is_it, d_weight, 0.0)

    for c in range(num):
        head_out[c, :STRETCH] = dqt_ref[:, part(c)].T
        head_out[c, STRETCH:] = dk_acc[part(c), :]

    def send_head(k, _):
        to = lax.rem(mine + k, n_head)
        pltpu.make_async_remote_copy(
            src_ref=head_out.at[to],
            dst_ref=head_in.at[mine],
            send_sem=sems.at[4],
            recv_sem=sems.at[5],
            device_id={"head": to},
        ).start()
        return 0

    lax.fori_loop(1, n_head, send_head, 0)
    head_in[mine] = head_out[mine]

    from_here = ones_where(row_at >= lane_at)
    terms = []
    for h in range(heads):
        for c in range(num):
            r = h * num + c
            term = query_terms[r] - key_terms[r]
            for level in range(LOCAL_LEVELS + 1, LOCAL_LEVELS + 1 + bits):
                term = term + w_ref[h, level : level + 1, part(c)] * dw_ref[
                    h, level : level + 1, part(c)
                ]
            terms.append(term)
    terms = jnp.concatenate(terms, axis=0)
    suffix = sum_of([dot(x, from_here) for x in thirds(terms)])
    sums = jnp.broadcast_to(suffix[:, :1], suffix.shape)
    suffix = suffix + sum_of([dot(later, x) for x in thirds(sums)])
    for h in range(heads):
        beyond = sum_of([buf2[(h * per_head + i) * slabs + 1] for i in range(per_head)])
        beyond = jnp.sum(jnp.sum(beyond, axis=0, keepdims=True), axis=1, keepdims=True)
        for c in range(num):
            r = h * num + c
            dg_ref[h : h + 1, part(c)] = suffix[r : r + 1] + beyond

    for size in range(bits + 1):

        @pl.when(count == size)
        def _(size=size):
            sent = out1.at[pl.ds(0, (n_ctx - 1) * (EXTRA + size))]
            pltpu.make_async_copy(sent, sent, sems.at[0]).wait()
            sent = out2.at[pl.ds(0, everything - EXTRA - size)]
            pltpu.make_async_copy(sent, sent, sems.at[2]).wait()

    others = head_in.at[pl.ds(0, n_head - 1)]
    pltpu.make_async_copy(others, others, sems.at[5]).wait()
    pltpu.make_async_copy(others, others, sems.at[4]).wait()
    dq_ref[...] = sum_of([head_in[n, :STRETCH] for n in range(n_head)])
    dk_ref[...] = sum_of([head_in[n, STRETCH:] for n in range(n_head)])


def shards(queries, keys, values, gates, level_weights, segment, cotangent):
    n_ctx, n_head = lax.axis_size("ctx"), lax.axis_size("head")
    heads, tokens = gates.shape
    num = tokens // STRETCH
    bits = n_ctx.bit_length() - 1
    slab_rows = heads * STRETCH // n_ctx
    held = pltpu.VMEM((n_ctx * (EXTRA + bits), slab_rows, STRETCH), F32)
    turned = pltpu.VMEM((STRETCH, tokens), F32)
    turned_half = pltpu.VMEM((STRETCH, tokens), BF16)
    chunks = pltpu.VMEM((n_head, 2 * STRETCH, STRETCH), F32)
    vmem = pl.BlockSpec(memory_space=pltpu.VMEM)
    rows_out = tokens // n_head
    return pl.pallas_call(
        functools.partial(kernel, n_ctx, n_head),
        out_shape=(
            jax.ShapeDtypeStruct((rows_out, STRETCH), F32),
            jax.ShapeDtypeStruct((rows_out, STRETCH), F32),
            jax.ShapeDtypeStruct(values.shape, F32),
            jax.ShapeDtypeStruct(gates.shape, F32),
            jax.ShapeDtypeStruct(level_weights.shape, F32),
        ),
        in_specs=[vmem] * 7,
        out_specs=(vmem,) * 5,
        scratch_shapes=[
            turned,
            turned,
            turned_half,
            turned_half,
            pltpu.VMEM((heads, STRETCH, tokens), BF16),
            pltpu.VMEM((heads, num, STRETCH, STRETCH), F32),
            held,
            held,
            held,
            held,
            turned,
            pltpu.VMEM((tokens, STRETCH), F32),
            chunks,
            chunks,
            pltpu.SemaphoreType.DMA((6,)),
        ],
        compiler_params=pltpu.CompilerParams(
            collective_id=0, has_side_effects=True, vmem_limit_bytes=40 * 2**20
        ),
        name="loglinear_backward",
    )(
        queries,
        keys,
        values,
        cotangent,
        gates,
        level_weights,
        segment.reshape(num, STRETCH),
    )


def solution(mesh):
    return jax.shard_map(
        shards,
        mesh=mesh,
        in_specs=(
            P("ctx", None),
            P("ctx", None),
            P("ctx", "head"),
            P("head", "ctx"),
            P("head", None, "ctx"),
            P("ctx"),
            P("ctx", "head"),
        ),
        out_specs=(
            P(("ctx", "head"), None),
            P(("ctx", "head"), None),
            P("ctx", "head"),
            P("head", "ctx"),
            P("head", None, "ctx"),
        ),
        check_vma=False,
    )
```

```python
import functools

import jax
import jax.numpy as jnp
from jax import lax
from jax.experimental import pallas as pl
from jax.experimental.pallas import tpu as pltpu
from jax.sharding import PartitionSpec as P

STRETCH = 128
LOCAL_LEVELS = 3
EXTRA = 1
F32 = jnp.float32
BF16 = jnp.bfloat16


def halves(x):
    high = x.astype(BF16)
    return high, (x - high.astype(F32)).astype(BF16)


def thirds(x):
    high = x.astype(BF16)
    rest = x - high.astype(F32)
    middle = rest.astype(BF16)
    return high, middle, (rest - middle.astype(F32)).astype(BF16)


def dot(a, b):
    return jnp.dot(a, b, preferred_element_type=F32)


def dot_nt(a, b):
    return lax.dot_general(a, b, (((1,), (1,)), ((), ())), preferred_element_type=F32)


def dot_left(x, exact):
    high, low = halves(x)
    return dot(high, exact) + dot(low, exact)


def dot_right(exact, x):
    high, low = halves(x)
    return dot(exact, high) + dot(exact, low)


def sum_of(terms):
    return functools.reduce(jnp.add, terms)


def ones_where(mask):
    return jnp.where(mask, 1.0, 0.0).astype(BF16)


def part(c):
    return slice(c * STRETCH, (c + 1) * STRETCH)


def pop(number, bits):
    return sum_of([(number >> b) & 1 for b in range(bits)])


def kernel(
    n_ctx,
    n_head,
    q_in,
    k_in,
    v_in,
    c_in,
    g_in,
    w_in,
    s_in,
    dq_out,
    dk_out,
    dv_out,
    dg_out,
    dw_out,
    dq_ref,
    dk_ref,
    dv_ref,
    dg_ref,
    dw_ref,
    q_ref,
    k_ref,
    v_ref,
    c_ref,
    g_ref,
    w_ref,
    s_ref,
    qt_ref,
    kt_ref,
    qtb_ref,
    ktb_ref,
    ctb_ref,
    block_ref,
    out1,
    buf1,
    out2,
    buf2,
    dqt_ref,
    dk_acc,
    meta_out,
    meta_in,
    flow_out,
    flow_in,
    head_out,
    pair_in,
    head_in,
    sems,
    pair_sems,
    in_sems,
    out_sems,
):
    loads = [
        pltpu.make_async_copy(source, target, in_sems.at[i])
        for i, (source, target) in enumerate(
            [
                (g_in, g_ref),
                (s_in, s_ref),
                (k_in, k_ref),
                (v_in, v_ref),
                (q_in, q_ref),
                (c_in, c_ref),
                (w_in, w_ref),
            ]
        )
    ]
    for load in loads:
        load.start()
    heads, tokens = g_ref.shape
    num = tokens // STRETCH
    rows = heads * num
    bits = n_ctx.bit_length() - 1
    slabs = EXTRA + bits
    slab_rows = buf1.shape[1]
    per_head = n_ctx // heads
    me = lax.axis_index("ctx")
    mine = lax.axis_index("head")
    count = pop(me, bits)
    everything = sum(EXTRA + bin(n).count("1") for n in range(n_ctx))

    barrier = pltpu.get_barrier_semaphore()

    def greet_ctx(k, _):
        pl.semaphore_signal(barrier, inc=1, device_id={"ctx": lax.rem(me + k, n_ctx)})
        return 0

    def greet_head(k, _):
        pl.semaphore_signal(barrier, inc=1, device_id={"head": lax.rem(mine + k, n_head)})
        return 0

    lax.fori_loop(1, n_ctx, greet_ctx, 0)
    lax.fori_loop(1, n_head, greet_head, 0)

    for load in loads[:2]:
        load.wait()

    gates = jnp.concatenate(
        [g_ref[h : h + 1, part(c)] for h in range(heads) for c in range(num)], axis=0
    )
    seg_one = s_ref[...]
    seg = jnp.concatenate([seg_one] * heads, axis=0)
    row_at = lax.broadcasted_iota(jnp.int32, (STRETCH, STRETCH), 0)
    lane_at = lax.broadcasted_iota(jnp.int32, (STRETCH, STRETCH), 1)
    upto = ones_where(row_at <= lane_at)
    within = sum_of([dot(x, upto) for x in thirds(gates)])
    total = jnp.broadcast_to(within[:, STRETCH - 1 :], within.shape)
    seg_end = jnp.broadcast_to(seg[:, STRETCH - 1 :], seg.shape)
    seg_first = jnp.broadcast_to(seg_one[:, :1], seg_one.shape)[:1]
    ra = lax.broadcasted_iota(jnp.int32, (rows, rows), 0)
    rb = lax.broadcasted_iota(jnp.int32, (rows, rows), 1)
    same_head = (ra // num) == (rb // num)
    earlier = ones_where(same_head & (rb < ra))
    later = ones_where(same_head & (rb > ra))
    before = sum_of([dot(earlier, x) for x in thirds(total)])
    entry = jnp.where(seg == seg_first, jnp.exp(within + before), 0.0)
    key_weight = jnp.where(seg == seg_end, jnp.exp(total - within), 0.0)
    through_exp = jnp.exp(total)

    def end(c):
        return seg_end[c : c + 1]

    def through(h, c):
        r = h * num + c
        return jnp.where(end(c - 1) == end(c), through_exp[r : r + 1], 0.0)

    def local_weight(h, level, c):
        r = h * num + c
        span = 1 << (level - 1)
        base = c // span * span
        shift = before[r : r + 1] - before[h * num + base : h * num + base + 1]
        return jnp.where(
            seg[r : r + 1] == end(base - 1), jnp.exp(within[r : r + 1] + shift), 0.0
        )

    def remote_row(h, k, c):
        picked = jnp.zeros((1, STRETCH), F32)
        for b in range(bits):
            is_it = (((me >> b) & 1) == 1) & (pop(me & ((1 << b) - 1), bits) == k)
            level = LOCAL_LEVELS + 1 + b
            picked = picked + jnp.where(is_it, w_ref[level, h : h + 1, part(c)], 0.0)
        return picked

    def columns(ref, h):
        return ref[:, h * STRETCH : (h + 1) * STRETCH]

    for load in loads[2:]:
        load.wait()

    qt_ref[...] = q_ref[...].astype(F32).T
    kt_ref[...] = k_ref[...].astype(F32).T
    qtb_ref[...] = qt_ref[...].astype(BF16)
    ktb_ref[...] = kt_ref[...].astype(BF16)
    for h in range(heads):
        ctb_ref[h] = columns(c_ref, h).astype(F32).T.astype(BF16)

    for h in range(heads):
        for c in range(num):
            r = h * num + c
            scaled = kt_ref[:, part(c)] * key_weight[r : r + 1]
            block_ref[h, c] = dot_left(scaled, v_ref[part(c), h * STRETCH : (h + 1) * STRETCH])
        state = block_ref[h, 0]
        for c in range(1, num):
            state = through(h, c) * state + block_ref[h, c]
        last = h * num + num - 1
        passes = jnp.where(
            seg_first == end(num - 1), jnp.exp(before[last : last + 1] + total[last : last + 1]), 0.0
        )
        at = lax.broadcasted_iota(jnp.int32, (1, STRETCH), 1)
        meta_out[h] = jnp.where(
            at < 32,
            passes,
            jnp.where(at < 64, seg_first.astype(F32), end(num - 1).astype(F32)),
        )
        for i in range(per_head):
            to = (h * per_head + i) * slabs
            out1[to] = state[i * slab_rows : (i + 1) * slab_rows]

    for k in range(bits):

        @pl.when(count > k)
        def _(k=k):
            for h in range(heads):
                scaled = jnp.concatenate(
                    [
                        qt_ref[:, part(c)]
                        * (entry[h * num + c : h * num + c + 1] * remote_row(h, k, c))
                        for c in range(num)
                    ],
                    axis=1,
                )
                grad = dot_left(scaled, columns(c_ref, h))
                for i in range(per_head):
                    out1[(h * per_head + i) * slabs + EXTRA + k] = grad[
                        i * slab_rows : (i + 1) * slab_rows
                    ]

    pl.semaphore_wait(barrier, n_ctx + n_head - 2)

    def send_meta(k, _):
        to = lax.rem(me + k, n_ctx)
        pltpu.make_async_remote_copy(
            src_ref=meta_out.at[to // per_head],
            dst_ref=meta_in.at[me],
            send_sem=sems.at[6],
            recv_sem=sems.at[7],
            device_id={"ctx": to},
        ).start()
        return 0

    lax.fori_loop(1, n_ctx, send_meta, 0)
    meta_in[me] = meta_out[me // per_head]

    for size in range(bits + 1):

        @pl.when(count == size)
        def _(size=size):
            def send(k, _):
                to = lax.rem(me + k, n_ctx)
                pltpu.make_async_remote_copy(
                    src_ref=out1.at[pl.ds(to * slabs, EXTRA + size)],
                    dst_ref=buf1.at[pl.ds(me * slabs, EXTRA + size)],
                    send_sem=sems.at[0],
                    recv_sem=sems.at[1],
                    device_id={"ctx": to},
                ).start()
                return 0

            lax.fori_loop(1, n_ctx, send, 0)
            for s in range(EXTRA + size):
                buf1[me * slabs + s] = out1[me * slabs + s]

    ones = jnp.ones((8, STRETCH), BF16)
    key_terms = [None] * rows
    query_terms = [None] * rows
    for c in range(num):
        seg_row = seg_one[c : c + 1]
        seg_col = jnp.broadcast_to(seg_row.astype(F32), (STRETCH, STRETCH)).T
        allowed = (row_at <= lane_at) & (seg_col == seg_row.astype(F32))
        scores = dot(k_ref[part(c), :], qtb_ref[:, part(c)])
        dk_sum = None
        dq_sum = None
        for h in range(heads):
            r = h * num + c
            cols = slice(h * STRETCH, (h + 1) * STRETCH)
            w_row = within[r : r + 1]
            w_col = jnp.broadcast_to(w_row, (STRETCH, STRETCH)).T
            decay = jnp.where(allowed, jnp.exp(jnp.minimum(w_row - w_col, 0.0)), 0.0)
            pairs = dot(v_ref[part(c), cols], ctb_ref[h, :, part(c)])
            mixed = decay * scores
            weight = w_ref[0, h : h + 1, part(c)]
            d_weight = jnp.sum(mixed * pairs, axis=0, keepdims=True)
            dw_ref[0, h : h + 1, part(c)] = d_weight
            query_terms[r] = weight * d_weight
            dv_ref[part(c), cols] = dot_left(mixed * weight, c_ref[part(c), cols])
            d_scores = decay * pairs * weight
            dk_one = dot_left(d_scores, q_ref[part(c), :])
            dq_one = dot_right(ktb_ref[:, part(c)], d_scores)
            products = k_ref[part(c), :].astype(F32) * dk_one
            key_terms[r] = sum_of([dot_nt(ones, x) for x in thirds(products)])[:1]
            dk_sum = dk_one if dk_sum is None else dk_sum + dk_one
            dq_sum = dq_one if dq_sum is None else dq_sum + dq_one
        dk_acc[part(c), :] = dk_sum
        dqt_ref[:, part(c)] = dq_sum

    for size in range(bits + 1):

        @pl.when(count == size)
        def _(size=size):
            got = buf1.at[pl.ds(0, everything - EXTRA - size)]
            pltpu.make_async_copy(got, got, sems.at[1]).wait()

    got_meta = meta_in.at[pl.ds(0, n_ctx - 1)]
    pltpu.make_async_copy(got_meta, got_meta, sems.at[7]).wait()
    meta_rows = [
        [jnp.broadcast_to(meta_in[n][:, i : i + 1], (1, STRETCH)) for i in (0, 32, 64)]
        for n in range(n_ctx)
    ]
    enter = [None] + [
        jnp.where(meta_rows[n - 1][2] == meta_rows[n][1], 1.0, 0.0) for n in range(1, n_ctx)
    ]
    link = [jnp.zeros_like(meta_rows[0][0])] + [
        meta_rows[n][0] * enter[n] for n in range(1, n_ctx)
    ]

    def received(n, s):
        return buf1[n * slabs + s]

    def rank(n, b):
        return bin(n & ((1 << b) - 1)).count("1")

    blocks = [[received(n, 0) for n in range(n_ctx)]]
    passing = [link]
    for b in range(bits):
        low, thru = blocks[b], passing[b]
        half = len(low) // 2
        blocks.append([thru[2 * j + 1] * low[2 * j] + low[2 * j + 1] for j in range(half)])
        passing.append([thru[2 * j] * thru[2 * j + 1] for j in range(half)])
    block_grads = [[None] * (n_ctx >> b) for b in range(bits)]
    flows = [jnp.zeros((slab_rows, STRETCH), F32)] * n_ctx
    for b in range(bits):
        for j in range(1, n_ctx >> b, 2):
            lead = None
            for p in range(j << b, (j + 1) << b):
                lead = jnp.ones((1, STRETCH), F32) if lead is None else lead * link[p - 1]
                factor = lead * enter[p]
                remote = factor * blocks[b][j - 1]
                slot = EXTRA + rank(p, b)
                out2[p * slabs + slot] = remote
                grad = received(p, slot)
                flows[p] = flows[p] + remote * grad
                term = factor * grad
                old = block_grads[b][j - 1]
                block_grads[b][j - 1] = term if old is None else old + term
    down = [jnp.zeros((slab_rows, STRETCH), F32)]
    for b in reversed(range(bits)):
        next_down = []
        for j, top in enumerate(down):
            next_down += [block_grads[b][2 * j] + passing[b][2 * j + 1] * top, top]
        down = next_down
    after = jnp.zeros((slab_rows, STRETCH), F32)
    for n in reversed(range(n_ctx)):
        out2[n * slabs] = down[n]
        flow_out[n] = jnp.sum(after, axis=0, keepdims=True)
        after = after + (flows[n] - received(n, 0) * down[n])

    def send_back(k, _):
        to = lax.rem(me + k, n_ctx)
        pltpu.make_async_remote_copy(
            src_ref=flow_out.at[to],
            dst_ref=flow_in.at[me],
            send_sem=sems.at[8],
            recv_sem=sems.at[9],
            device_id={"ctx": to},
        ).start()
        size_there = pop(to, bits)
        for size in range(bits + 1):

            @pl.when(size_there == size)
            def _(size=size):
                pltpu.make_async_remote_copy(
                    src_ref=out2.at[pl.ds(to * slabs, EXTRA + size)],
                    dst_ref=buf2.at[pl.ds(me * slabs, EXTRA + size)],
                    send_sem=sems.at[2],
                    recv_sem=sems.at[3],
                    device_id={"ctx": to},
                ).start()

        return 0

    lax.fori_loop(1, n_ctx, send_back, 0)
    flow_in[me] = flow_out[me]
    for size in range(bits + 1):

        @pl.when(count == size)
        def _(size=size):
            for s in range(EXTRA + size):
                buf2[me * slabs + s] = out2[me * slabs + s]

    state_grads = []
    for h in range(heads):
        cols = slice(h * STRETCH, (h + 1) * STRETCH)
        lower = [block_ref[h, c] for c in range(num)]
        thru = [None] + [through(h, c) for c in range(1, num)]
        thru[0] = jnp.zeros_like(thru[1])
        per_level = []
        thrus = []
        for level in range(1, LOCAL_LEVELS + 1):
            span = 1 << (level - 1)
            grads = [None] * len(lower)
            for j in range(1, len(lower), 2):
                lanes = slice(j * span * STRETCH, (j + 1) * span * STRETCH)
                high, low = halves(lower[j - 1])
                reach = ctb_ref[h, :, lanes]
                got = dot(high, reach) + dot(low, reach)
                scaled = []
                for c in range(j * span, (j + 1) * span):
                    r = h * num + c
                    here = slice((c - j * span) * STRETCH, (c - j * span + 1) * STRETCH)
                    decay = local_weight(h, level, c)
                    q_part = qt_ref[:, part(c)]
                    d_weight = decay * jnp.sum(q_part * got[:, here], axis=0, keepdims=True)
                    weight = w_ref[level, h : h + 1, part(c)]
                    dw_ref[level, h : h + 1, part(c)] = d_weight
                    query_terms[r] = query_terms[r] + weight * d_weight
                    both = weight * decay
                    dqt_ref[:, part(c)] += both * got[:, here]
                    scaled.append(q_part * both)
                scaled = jnp.concatenate(scaled, axis=1) if span > 1 else scaled[0]
                grads[j - 1] = dot_left(scaled, c_ref[lanes, cols])
            for j in range(0, len(lower), 2):
                for c in range(j * span, (j + 1) * span):
                    dw_ref[level, h : h + 1, part(c)] = jnp.zeros((1, STRETCH), F32)
            per_level.append(grads)
            thrus.append(thru)
            lower, thru = (
                [thru[j + 1] * lower[j] + lower[j + 1] for j in range(0, len(lower), 2)],
                [thru[j] * thru[j + 1] for j in range(0, len(lower), 2)],
            )
        down = [None]
        for level in reversed(range(LOCAL_LEVELS)):
            next_down = []
            for j, top in enumerate(down):
                low = per_level[level][2 * j]
                next_down += [low if top is None else low + thrus[level][2 * j + 1] * top, top]
            down = next_down
        for c in range(num - 1):
            block_ref[h, c] = down[c]
        block_ref[h, num - 1] = jnp.zeros((STRETCH, STRETCH), F32)
        state_grads.append(None)

    for size in range(bits + 1):

        @pl.when(count == size)
        def _(size=size):
            got = buf2.at[pl.ds(0, (n_ctx - 1) * (EXTRA + size))]
            pltpu.make_async_copy(got, got, sems.at[3]).wait()

    def gathered(h, s):
        return jnp.concatenate(
            [buf2[(h * per_head + i) * slabs + s] for i in range(per_head)], axis=0
        )

    for h in range(heads):
        cols = slice(h * STRETCH, (h + 1) * STRETCH)
        top = gathered(h, 0)
        for c in reversed(range(num)):
            r = h * num + c
            seg_col = jnp.broadcast_to(seg_one[c : c + 1].astype(F32), (STRETCH, STRETCH)).T
            w_col = jnp.broadcast_to(within[r : r + 1], (STRETCH, STRETCH)).T
            weight = jnp.where(
                seg_col == end(c).astype(F32), jnp.exp(total[r : r + 1] - w_col), 0.0
            )
            high, low = halves(block_ref[h, c] + top)
            keys_here = k_ref[part(c), :]
            values_here = v_ref[part(c), cols]
            dv_ref[part(c), cols] += weight * (dot(keys_here, high) + dot(keys_here, low))
            dk_one = weight * (dot_nt(values_here, high) + dot_nt(values_here, low))
            dk_acc[part(c), :] += dk_one
            products = keys_here.astype(F32) * dk_one
            key_terms[r] = (
                key_terms[r] + sum_of([dot_nt(ones, x) for x in thirds(products)])[:1]
            )
            if c:
                top = through(h, c) * top

    dw_ref[LOCAL_LEVELS + 1 :] = jnp.zeros(
        (dw_ref.shape[0] - LOCAL_LEVELS - 1, heads, tokens), F32
    )
    for k in range(bits):

        @pl.when(count > k)
        def _(k=k):
            for h in range(heads):
                high, low = halves(gathered(h, EXTRA + k))
                for c in range(num):
                    reach = ctb_ref[h, :, part(c)]
                    got = dot(high, reach) + dot(low, reach)
                    decay = entry[h * num + c : h * num + c + 1]
                    d_weight = decay * jnp.sum(qt_ref[:, part(c)] * got, axis=0, keepdims=True)
                    dqt_ref[:, part(c)] += (decay * remote_row(h, k, c)) * got
                    for b in range(bits):
                        is_it = (((me >> b) & 1) == 1) & (pop(me & ((1 << b) - 1), bits) == k)
                        level = LOCAL_LEVELS + 1 + b
                        dw_ref[level, h : h + 1, part(c)] += jnp.where(is_it, d_weight, 0.0)

    def store(i, source, target):
        copy = pltpu.make_async_copy(source, target, out_sems.at[i])
        copy.start()
        return copy

    stores = [store(2, dv_ref, dv_out), store(4, dw_ref, dw_out)]

    for c in range(num):
        head_out[c, :STRETCH] = dqt_ref[:, part(c)].T
        head_out[c, STRETCH:] = dk_acc[part(c), :]

    n_chip = n_head // 2
    core, chip = lax.rem(mine, 2), mine // 2
    sibling = chip * 2 + 1 - core
    for x in range(n_chip):
        pltpu.make_async_remote_copy(
            src_ref=head_out.at[2 * x + 1 - core],
            dst_ref=pair_in.at[x],
            send_sem=pair_sems.at[0, x],
            recv_sem=pair_sems.at[1, x],
            device_id={"head": sibling},
        ).start()

    def join(x):
        pltpu.make_async_copy(pair_in.at[x], pair_in.at[x], pair_sems.at[1, x]).wait()
        pair_in[x] = pair_in[x] + head_out[2 * x + core]

    for k in range(1, n_chip):
        x = lax.rem(chip + k, n_chip)
        join(x)
        pltpu.make_async_remote_copy(
            src_ref=pair_in.at[x],
            dst_ref=head_in.at[chip],
            send_sem=sems.at[4],
            recv_sem=sems.at[5],
            device_id={"head": x * 2 + core},
        ).start()
    join(chip)
    head_in[chip] = pair_in[chip]

    got_flow = flow_in.at[pl.ds(0, n_ctx - 1)]
    pltpu.make_async_copy(got_flow, got_flow, sems.at[9]).wait()
    from_here = ones_where(row_at >= lane_at)
    terms = []
    for h in range(heads):
        for c in range(num):
            r = h * num + c
            term = query_terms[r] - key_terms[r]
            for level in range(LOCAL_LEVELS + 1, LOCAL_LEVELS + 1 + bits):
                term = term + w_ref[level, h : h + 1, part(c)] * dw_ref[
                    level, h : h + 1, part(c)
                ]
            terms.append(term)
    terms = jnp.concatenate(terms, axis=0)
    suffix = sum_of([dot(x, from_here) for x in thirds(terms)])
    sums = jnp.broadcast_to(suffix[:, :1], suffix.shape)
    suffix = suffix + sum_of([dot(later, x) for x in thirds(sums)])
    for h in range(heads):
        beyond = sum_of([flow_in[h * per_head + i] for i in range(per_head)])
        beyond = jnp.sum(beyond, axis=1, keepdims=True)
        for c in range(num):
            r = h * num + c
            dg_ref[h : h + 1, part(c)] = suffix[r : r + 1] + beyond
    stores.append(store(3, dg_ref, dg_out))

    for size in range(bits + 1):

        @pl.when(count == size)
        def _(size=size):
            sent = out1.at[pl.ds(0, (n_ctx - 1) * (EXTRA + size))]
            pltpu.make_async_copy(sent, sent, sems.at[0]).wait()
            sent = out2.at[pl.ds(0, everything - EXTRA - size)]
            pltpu.make_async_copy(sent, sent, sems.at[2]).wait()

    sent = meta_in.at[pl.ds(0, n_ctx - 1)]
    pltpu.make_async_copy(sent, sent, sems.at[6]).wait()
    pltpu.make_async_copy(sent, sent, sems.at[8]).wait()
    for x in range(n_chip):
        pltpu.make_async_copy(pair_in.at[x], pair_in.at[x], pair_sems.at[0, x]).wait()

    others = head_in.at[pl.ds(0, n_chip - 1)]
    pltpu.make_async_copy(others, others, sems.at[5]).wait()
    pltpu.make_async_copy(others, others, sems.at[4]).wait()
    dq_ref[...] = sum_of([head_in[n, :STRETCH] for n in range(n_chip)])
    dk_ref[...] = sum_of([head_in[n, STRETCH:] for n in range(n_chip)])
    stores.append(store(0, dq_ref, dq_out))
    stores.append(store(1, dk_ref, dk_out))
    for copy in stores:
        copy.wait()


def finish(pieces, *refs):
    half = len(pieces)
    given, results, held = refs[:half], refs[half : 2 * half], refs[2 * half : 3 * half]
    load_sems, store_sems = refs[3 * half :]
    steps = []
    for ref, out, mid, count in zip(given, results, held, pieces):
        size = ref.shape[0] // count
        for at in range(count):
            cut = pl.ds(at * size, size)
            i = len(steps)
            steps.append(
                (
                    pltpu.make_async_copy(ref.at[cut], mid.at[cut], load_sems.at[i]),
                    pltpu.make_async_copy(mid.at[cut], out.at[cut], store_sems.at[i]),
                )
            )
    for load, _ in steps:
        load.start()
    for load, store in steps:
        load.wait()
        store.start()
    for _, store in steps:
        store.wait()


def shards(queries, keys, values, gates, level_weights, segment, cotangent):
    n_ctx, n_head = lax.axis_size("ctx"), lax.axis_size("head")
    heads, tokens = gates.shape
    num = tokens // STRETCH
    bits = n_ctx.bit_length() - 1
    slab_rows = heads * STRETCH // n_ctx
    held = pltpu.VMEM((n_ctx * (EXTRA + bits), slab_rows, STRETCH), F32)
    turned = pltpu.VMEM((STRETCH, tokens), F32)
    turned_half = pltpu.VMEM((STRETCH, tokens), BF16)

    def chunks(n):
        return pltpu.VMEM((n, 2 * STRETCH, STRETCH), F32)

    anywhere = pl.BlockSpec(memory_space=pl.ANY)
    rows_out = tokens // n_head
    weights = level_weights.transpose(1, 0, 2)
    segments = segment.reshape(num, STRETCH)
    inputs = (queries, keys, values, cotangent, gates, weights, segments)
    results = (
        jax.ShapeDtypeStruct((rows_out, STRETCH), F32),
        jax.ShapeDtypeStruct((rows_out, STRETCH), F32),
        jax.ShapeDtypeStruct(values.shape, F32),
        jax.ShapeDtypeStruct(gates.shape, F32),
        jax.ShapeDtypeStruct(weights.shape, F32),
    )
    raw = pl.pallas_call(
        functools.partial(kernel, n_ctx, n_head),
        out_shape=results,
        in_specs=[anywhere] * 7,
        out_specs=(anywhere,) * 5,
        scratch_shapes=[
            *[pltpu.VMEM(x.shape, x.dtype) for x in (*results, *inputs)],
            turned,
            turned,
            turned_half,
            turned_half,
            pltpu.VMEM((heads, STRETCH, tokens), BF16),
            pltpu.VMEM((heads, num, STRETCH, STRETCH), F32),
            held,
            held,
            held,
            held,
            turned,
            pltpu.VMEM((tokens, STRETCH), F32),
            pltpu.VMEM((heads, 1, STRETCH), F32),
            pltpu.VMEM((n_ctx, 1, STRETCH), F32),
            pltpu.VMEM((n_ctx, 1, STRETCH), F32),
            pltpu.VMEM((n_ctx, 1, STRETCH), F32),
            chunks(n_head),
            chunks(n_head // 2),
            chunks(n_head // 2),
            pltpu.SemaphoreType.DMA((10,)),
            pltpu.SemaphoreType.DMA((2, n_head // 2)),
            pltpu.SemaphoreType.DMA((7,)),
            pltpu.SemaphoreType.DMA((5,)),
        ],
        compiler_params=pltpu.CompilerParams(
            collective_id=0, has_side_effects=True, vmem_limit_bytes=56 * 2**20
        ),
        name="loglinear_backward",
    )(*inputs)
    pieces = (1, 1, 4, 1, 1)
    *outs, weight_grad = pl.pallas_call(
        functools.partial(finish, pieces),
        out_shape=[jax.ShapeDtypeStruct(x.shape, F32) for x in raw],
        in_specs=[anywhere] * len(raw),
        out_specs=[anywhere] * len(raw),
        scratch_shapes=[
            *[pltpu.VMEM(x.shape, F32) for x in raw],
            pltpu.SemaphoreType.DMA((sum(pieces),)),
            pltpu.SemaphoreType.DMA((sum(pieces),)),
        ],
        name="store_results",
    )(*raw)
    return (*outs, weight_grad.transpose(1, 0, 2))


def solution(mesh):
    return jax.shard_map(
        shards,
        mesh=mesh,
        in_specs=(
            P("ctx", None),
            P("ctx", None),
            P("ctx", "head"),
            P("head", "ctx"),
            P("head", None, "ctx"),
            P("ctx"),
            P("ctx", "head"),
        ),
        out_specs=(
            P(("ctx", "head"), None),
            P(("ctx", "head"), None),
            P("ctx", "head"),
            P("head", "ctx"),
            P("head", None, "ctx"),
        ),
        check_vma=False,
    )
```

```python
import functools

import jax
import jax.numpy as jnp
from jax import lax
from jax.experimental import pallas as pl
from jax.experimental.pallas import tpu as pltpu
from jax.sharding import PartitionSpec as P

STRETCH = 128
LOCAL_LEVELS = 3
F32 = jnp.float32
BF16 = jnp.bfloat16


def halves(x):
    high = x.astype(BF16)
    return high, (x - high.astype(F32)).astype(BF16)


def thirds(x):
    high = x.astype(BF16)
    rest = x - high.astype(F32)
    middle = rest.astype(BF16)
    return high, middle, (rest - middle.astype(F32)).astype(BF16)


def dot(a, b):
    return jnp.dot(a, b, preferred_element_type=F32)


def dot_nt(a, b):
    return lax.dot_general(a, b, (((1,), (1,)), ((), ())), preferred_element_type=F32)


def dot_left(x, exact):
    high, low = halves(x)
    return dot(high, exact) + dot(low, exact)


def dot_right(exact, x):
    high, low = halves(x)
    return dot(exact, high) + dot(exact, low)


def sum_of(terms):
    return functools.reduce(jnp.add, terms)


def ones_where(mask):
    return jnp.where(mask, 1.0, 0.0).astype(BF16)


def part(c):
    return slice(c * STRETCH, (c + 1) * STRETCH)


def pop(number, bits):
    return sum_of([(number >> b) & 1 for b in range(bits)])


def kernel(
    n_ctx,
    n_head,
    q_in,
    k_in,
    v_in,
    c_in,
    g_in,
    w_in,
    s_in,
    dq_out,
    dk_out,
    dv_out,
    dg_out,
    dw_out,
    dq_ref,
    dk_ref,
    dv_ref,
    dg_ref,
    dw_ref,
    q_ref,
    k_ref,
    v_ref,
    c_ref,
    g_ref,
    w_ref,
    s_ref,
    qt_ref,
    kt_ref,
    qtb_ref,
    ktb_ref,
    ctb_ref,
    block_ref,
    s_out,
    s_in_buf,
    out1,
    buf1,
    out2,
    buf2,
    t_out,
    t_in,
    dqt_ref,
    dk_acc,
    meta_out,
    meta_in,
    flow_out,
    flow_in,
    head_out,
    pair_in,
    head_in,
    sems,
    pair_sems,
    in_sems,
    out_sems,
):
    loads = [
        pltpu.make_async_copy(source, target, in_sems.at[i])
        for i, (source, target) in enumerate(
            [
                (g_in, g_ref),
                (s_in, s_ref),
                (k_in, k_ref),
                (v_in, v_ref),
                (q_in, q_ref),
                (c_in, c_ref),
                (w_in, w_ref),
            ]
        )
    ]
    for load in loads:
        load.start()
    heads, tokens = g_ref.shape
    num = tokens // STRETCH
    rows = heads * num
    bits = n_ctx.bit_length() - 1
    slabs = bits
    slab_rows = buf1.shape[1]
    per_head = n_ctx // heads
    me = lax.axis_index("ctx")
    mine = lax.axis_index("head")
    count = pop(me, bits)
    everything = sum(bin(n).count("1") for n in range(n_ctx))

    def partner(k):
        step = (k + 1) // 2
        return lax.rem(jnp.where(lax.rem(k, 2) == 1, me + step, me + n_ctx - step), n_ctx)

    barrier = pltpu.get_barrier_semaphore()

    def greet_ctx(k, _):
        pl.semaphore_signal(barrier, inc=1, device_id={"ctx": lax.rem(me + k, n_ctx)})
        return 0

    def greet_head(k, _):
        pl.semaphore_signal(barrier, inc=1, device_id={"head": lax.rem(mine + k, n_head)})
        return 0

    lax.fori_loop(1, n_ctx, greet_ctx, 0)
    lax.fori_loop(1, n_head, greet_head, 0)

    for load in loads[:2]:
        load.wait()

    gates = jnp.concatenate(
        [g_ref[h : h + 1, part(c)] for h in range(heads) for c in range(num)], axis=0
    )
    seg_one = s_ref[...]
    seg = jnp.concatenate([seg_one] * heads, axis=0)
    row_at = lax.broadcasted_iota(jnp.int32, (STRETCH, STRETCH), 0)
    lane_at = lax.broadcasted_iota(jnp.int32, (STRETCH, STRETCH), 1)
    upto = ones_where(row_at <= lane_at)
    within = sum_of([dot(x, upto) for x in thirds(gates)])
    total = jnp.broadcast_to(within[:, STRETCH - 1 :], within.shape)
    seg_end = jnp.broadcast_to(seg[:, STRETCH - 1 :], seg.shape)
    seg_first = jnp.broadcast_to(seg_one[:, :1], seg_one.shape)[:1]
    ra = lax.broadcasted_iota(jnp.int32, (rows, rows), 0)
    rb = lax.broadcasted_iota(jnp.int32, (rows, rows), 1)
    same_head = (ra // num) == (rb // num)
    earlier = ones_where(same_head & (rb < ra))
    later = ones_where(same_head & (rb > ra))
    before = sum_of([dot(earlier, x) for x in thirds(total)])
    entry = jnp.where(seg == seg_first, jnp.exp(within + before), 0.0)
    key_weight = jnp.where(seg == seg_end, jnp.exp(total - within), 0.0)
    through_exp = jnp.exp(total)

    def end(c):
        return seg_end[c : c + 1]

    def through(h, c):
        r = h * num + c
        return jnp.where(end(c - 1) == end(c), through_exp[r : r + 1], 0.0)

    def local_weight(h, level, c):
        r = h * num + c
        span = 1 << (level - 1)
        base = c // span * span
        shift = before[r : r + 1] - before[h * num + base : h * num + base + 1]
        return jnp.where(
            seg[r : r + 1] == end(base - 1), jnp.exp(within[r : r + 1] + shift), 0.0
        )

    def remote_row(h, k, c):
        picked = jnp.zeros((1, STRETCH), F32)
        for b in range(bits):
            is_it = (((me >> b) & 1) == 1) & (pop(me & ((1 << b) - 1), bits) == k)
            level = LOCAL_LEVELS + 1 + b
            picked = picked + jnp.where(is_it, w_ref[level, h : h + 1, part(c)], 0.0)
        return picked

    def columns(ref, h):
        return ref[:, h * STRETCH : (h + 1) * STRETCH]

    for load in loads[2:]:
        load.wait()

    qt_ref[...] = q_ref[...].astype(F32).T
    kt_ref[...] = k_ref[...].astype(F32).T
    qtb_ref[...] = qt_ref[...].astype(BF16)
    ktb_ref[...] = kt_ref[...].astype(BF16)
    for h in range(heads):
        ctb_ref[h] = columns(c_ref, h).astype(F32).T.astype(BF16)

    for h in range(heads):
        for c in range(num):
            r = h * num + c
            scaled = kt_ref[:, part(c)] * key_weight[r : r + 1]
            block_ref[h, c] = dot_left(scaled, v_ref[part(c), h * STRETCH : (h + 1) * STRETCH])
        state = block_ref[h, 0]
        for c in range(1, num):
            state = through(h, c) * state + block_ref[h, c]
        last = h * num + num - 1
        passes = jnp.where(
            seg_first == end(num - 1), jnp.exp(before[last : last + 1] + total[last : last + 1]), 0.0
        )
        at = lax.broadcasted_iota(jnp.int32, (1, STRETCH), 1)
        meta_out[h] = jnp.where(
            at < 32,
            passes,
            jnp.where(at < 64, seg_first.astype(F32), end(num - 1).astype(F32)),
        )
        for i in range(per_head):
            s_out[h * per_head + i] = state[i * slab_rows : (i + 1) * slab_rows]

    pl.semaphore_wait(barrier, n_ctx + n_head - 2)

    def send_state(k, _):
        to = partner(k)
        pltpu.make_async_remote_copy(
            src_ref=meta_out.at[to // per_head],
            dst_ref=meta_in.at[me],
            send_sem=sems.at[6],
            recv_sem=sems.at[7],
            device_id={"ctx": to},
        ).start()
        pltpu.make_async_remote_copy(
            src_ref=s_out.at[to],
            dst_ref=s_in_buf.at[me],
            send_sem=sems.at[10],
            recv_sem=sems.at[11],
            device_id={"ctx": to},
        ).start()
        return 0

    lax.fori_loop(1, n_ctx, send_state, 0)
    meta_in[me] = meta_out[me // per_head]
    s_in_buf[me] = s_out[me]

    for k in range(bits):

        @pl.when(count > k)
        def _(k=k):
            for h in range(heads):
                scaled = jnp.concatenate(
                    [
                        qt_ref[:, part(c)]
                        * (entry[h * num + c : h * num + c + 1] * remote_row(h, k, c))
                        for c in range(num)
                    ],
                    axis=1,
                )
                grad = dot_left(scaled, columns(c_ref, h))
                for i in range(per_head):
                    out1[(h * per_head + i) * slabs + k] = grad[
                        i * slab_rows : (i + 1) * slab_rows
                    ]

    for size in range(1, bits + 1):

        @pl.when(count == size)
        def _(size=size):
            def send(k, _):
                to = partner(k)
                pltpu.make_async_remote_copy(
                    src_ref=out1.at[pl.ds(to * slabs, size)],
                    dst_ref=buf1.at[pl.ds(me * slabs, size)],
                    send_sem=sems.at[0],
                    recv_sem=sems.at[1],
                    device_id={"ctx": to},
                ).start()
                return 0

            lax.fori_loop(1, n_ctx, send, 0)
            for s in range(size):
                buf1[me * slabs + s] = out1[me * slabs + s]

    got_state = s_in_buf.at[pl.ds(0, n_ctx - 1)]
    pltpu.make_async_copy(got_state, got_state, sems.at[11]).wait()
    got_meta = meta_in.at[pl.ds(0, n_ctx - 1)]
    pltpu.make_async_copy(got_meta, got_meta, sems.at[7]).wait()
    meta_rows = [
        [jnp.broadcast_to(meta_in[n][:, i : i + 1], (1, STRETCH)) for i in (0, 32, 64)]
        for n in range(n_ctx)
    ]
    enter = [None] + [
        jnp.where(meta_rows[n - 1][2] == meta_rows[n][1], 1.0, 0.0) for n in range(1, n_ctx)
    ]
    link = [jnp.zeros_like(meta_rows[0][0])] + [
        meta_rows[n][0] * enter[n] for n in range(1, n_ctx)
    ]

    def rank(n, b):
        return bin(n & ((1 << b) - 1)).count("1")

    blocks = [s_in_buf[n] for n in range(n_ctx)]
    passing = [link]
    factors = {}
    for b in range(bits):
        thru = passing[b]
        for j in range(1, n_ctx >> b, 2):
            lead = None
            for p in range(j << b, (j + 1) << b):
                lead = jnp.ones((1, STRETCH), F32) if lead is None else lead * link[p - 1]
                factors[b, p] = lead * enter[p]
                out2[p * slabs + rank(p, b)] = factors[b, p] * blocks[j - 1]
        half = len(blocks) // 2
        blocks = [thru[2 * j + 1] * blocks[2 * j] + blocks[2 * j + 1] for j in range(half)]
        passing.append([thru[2 * j] * thru[2 * j + 1] for j in range(half)])

    def send_buckets(k, _):
        to = partner(k)
        size_there = pop(to, bits)
        for size in range(1, bits + 1):

            @pl.when(size_there == size)
            def _(size=size):
                pltpu.make_async_remote_copy(
                    src_ref=out2.at[pl.ds(to * slabs, size)],
                    dst_ref=buf2.at[pl.ds(me * slabs, size)],
                    send_sem=sems.at[2],
                    recv_sem=sems.at[3],
                    device_id={"ctx": to},
                ).start()

        return 0

    lax.fori_loop(1, n_ctx, send_buckets, 0)
    for size in range(1, bits + 1):

        @pl.when(count == size)
        def _(size=size):
            for s in range(size):
                buf2[me * slabs + s] = out2[me * slabs + s]

    ones = jnp.ones((8, STRETCH), BF16)
    key_terms = [None] * rows
    query_terms = [None] * rows
    for c in range(num):
        seg_row = seg_one[c : c + 1]
        seg_col = jnp.broadcast_to(seg_row.astype(F32), (STRETCH, STRETCH)).T
        allowed = (row_at <= lane_at) & (seg_col == seg_row.astype(F32))
        scores = dot(k_ref[part(c), :], qtb_ref[:, part(c)])
        dk_sum = None
        dq_sum = None
        for h in range(heads):
            r = h * num + c
            cols = slice(h * STRETCH, (h + 1) * STRETCH)
            w_row = within[r : r + 1]
            w_col = jnp.broadcast_to(w_row, (STRETCH, STRETCH)).T
            decay = jnp.where(allowed, jnp.exp(jnp.minimum(w_row - w_col, 0.0)), 0.0)
            pairs = dot(v_ref[part(c), cols], ctb_ref[h, :, part(c)])
            mixed = decay * scores
            weight = w_ref[0, h : h + 1, part(c)]
            d_weight = jnp.sum(mixed * pairs, axis=0, keepdims=True)
            dw_ref[0, h : h + 1, part(c)] = d_weight
            query_terms[r] = weight * d_weight
            dv_ref[part(c), cols] = dot_left(mixed * weight, c_ref[part(c), cols])
            d_scores = decay * pairs * weight
            dk_one = dot_left(d_scores, q_ref[part(c), :])
            dq_one = dot_right(ktb_ref[:, part(c)], d_scores)
            products = k_ref[part(c), :].astype(F32) * dk_one
            key_terms[r] = sum_of([dot_nt(ones, x) for x in thirds(products)])[:1]
            dk_sum = dk_one if dk_sum is None else dk_sum + dk_one
            dq_sum = dq_one if dq_sum is None else dq_sum + dq_one
        dk_acc[part(c), :] = dk_sum
        dqt_ref[:, part(c)] = dq_sum

    for size in range(bits + 1):

        @pl.when(count == size)
        def _(size=size):
            got = buf1.at[pl.ds(0, everything - size)]
            pltpu.make_async_copy(got, got, sems.at[1]).wait()

    block_grads = [[None] * (n_ctx >> b) for b in range(bits)]
    flows = [jnp.zeros((slab_rows, STRETCH), F32)] * n_ctx
    for b in range(bits):
        for j in range(1, n_ctx >> b, 2):
            for p in range(j << b, (j + 1) << b):
                slot = p * slabs + rank(p, b)
                grad = buf1[slot]
                flows[p] = flows[p] + out2[slot] * grad
                term = factors[b, p] * grad
                old = block_grads[b][j - 1]
                block_grads[b][j - 1] = term if old is None else old + term
    down = [jnp.zeros((slab_rows, STRETCH), F32)]
    for b in reversed(range(bits)):
        next_down = []
        for j, top in enumerate(down):
            next_down += [block_grads[b][2 * j] + passing[b][2 * j + 1] * top, top]
        down = next_down
    after = jnp.zeros((slab_rows, STRETCH), F32)
    for n in reversed(range(n_ctx)):
        t_out[n] = down[n]
        flow_out[n] = jnp.sum(after, axis=0, keepdims=True)
        after = after + (flows[n] - s_in_buf[n] * down[n])

    def send_grads(k, _):
        to = partner(k)
        pltpu.make_async_remote_copy(
            src_ref=t_out.at[to],
            dst_ref=t_in.at[me],
            send_sem=sems.at[12],
            recv_sem=sems.at[13],
            device_id={"ctx": to},
        ).start()
        pltpu.make_async_remote_copy(
            src_ref=flow_out.at[to],
            dst_ref=flow_in.at[me],
            send_sem=sems.at[8],
            recv_sem=sems.at[9],
            device_id={"ctx": to},
        ).start()
        return 0

    lax.fori_loop(1, n_ctx, send_grads, 0)
    t_in[me] = t_out[me]
    flow_in[me] = flow_out[me]

    state_grads = []
    for h in range(heads):
        cols = slice(h * STRETCH, (h + 1) * STRETCH)
        lower = [block_ref[h, c] for c in range(num)]
        thru = [None] + [through(h, c) for c in range(1, num)]
        thru[0] = jnp.zeros_like(thru[1])
        per_level = []
        thrus = []
        for level in range(1, LOCAL_LEVELS + 1):
            span = 1 << (level - 1)
            grads = [None] * len(lower)
            for j in range(1, len(lower), 2):
                lanes = slice(j * span * STRETCH, (j + 1) * span * STRETCH)
                high, low = halves(lower[j - 1])
                reach = ctb_ref[h, :, lanes]
                got = dot(high, reach) + dot(low, reach)
                scaled = []
                for c in range(j * span, (j + 1) * span):
                    r = h * num + c
                    here = slice((c - j * span) * STRETCH, (c - j * span + 1) * STRETCH)
                    decay = local_weight(h, level, c)
                    q_part = qt_ref[:, part(c)]
                    d_weight = decay * jnp.sum(q_part * got[:, here], axis=0, keepdims=True)
                    weight = w_ref[level, h : h + 1, part(c)]
                    dw_ref[level, h : h + 1, part(c)] = d_weight
                    query_terms[r] = query_terms[r] + weight * d_weight
                    both = weight * decay
                    dqt_ref[:, part(c)] += both * got[:, here]
                    scaled.append(q_part * both)
                scaled = jnp.concatenate(scaled, axis=1) if span > 1 else scaled[0]
                grads[j - 1] = dot_left(scaled, c_ref[lanes, cols])
            for j in range(0, len(lower), 2):
                for c in range(j * span, (j + 1) * span):
                    dw_ref[level, h : h + 1, part(c)] = jnp.zeros((1, STRETCH), F32)
            per_level.append(grads)
            thrus.append(thru)
            lower, thru = (
                [thru[j + 1] * lower[j] + lower[j + 1] for j in range(0, len(lower), 2)],
                [thru[j] * thru[j + 1] for j in range(0, len(lower), 2)],
            )
        down = [None]
        for level in reversed(range(LOCAL_LEVELS)):
            next_down = []
            for j, top in enumerate(down):
                low = per_level[level][2 * j]
                next_down += [low if top is None else low + thrus[level][2 * j + 1] * top, top]
            down = next_down
        for c in range(num - 1):
            block_ref[h, c] = down[c]
        block_ref[h, num - 1] = jnp.zeros((STRETCH, STRETCH), F32)
        state_grads.append(None)

    for size in range(1, bits + 1):

        @pl.when(count == size)
        def _(size=size):
            got = buf2.at[pl.ds(0, (n_ctx - 1) * size)]
            pltpu.make_async_copy(got, got, sems.at[3]).wait()

    def gathered(ref, stride, s, h):
        return jnp.concatenate(
            [ref[(h * per_head + i) * stride + s] for i in range(per_head)], axis=0
        )

    dw_ref[LOCAL_LEVELS + 1 :] = jnp.zeros(
        (dw_ref.shape[0] - LOCAL_LEVELS - 1, heads, tokens), F32
    )
    for k in range(bits):

        @pl.when(count > k)
        def _(k=k):
            for h in range(heads):
                high, low = halves(gathered(buf2, slabs, k, h))
                for c in range(num):
                    reach = ctb_ref[h, :, part(c)]
                    got = dot(high, reach) + dot(low, reach)
                    decay = entry[h * num + c : h * num + c + 1]
                    d_weight = decay * jnp.sum(qt_ref[:, part(c)] * got, axis=0, keepdims=True)
                    dqt_ref[:, part(c)] += (decay * remote_row(h, k, c)) * got
                    for b in range(bits):
                        is_it = (((me >> b) & 1) == 1) & (pop(me & ((1 << b) - 1), bits) == k)
                        level = LOCAL_LEVELS + 1 + b
                        dw_ref[level, h : h + 1, part(c)] += jnp.where(is_it, d_weight, 0.0)

    got_grads = t_in.at[pl.ds(0, n_ctx - 1)]
    pltpu.make_async_copy(got_grads, got_grads, sems.at[13]).wait()

    for h in range(heads):
        cols = slice(h * STRETCH, (h + 1) * STRETCH)
        top = gathered(t_in, 1, 0, h)
        for c in reversed(range(num)):
            r = h * num + c
            seg_col = jnp.broadcast_to(seg_one[c : c + 1].astype(F32), (STRETCH, STRETCH)).T
            w_col = jnp.broadcast_to(within[r : r + 1], (STRETCH, STRETCH)).T
            weight = jnp.where(
                seg_col == end(c).astype(F32), jnp.exp(total[r : r + 1] - w_col), 0.0
            )
            high, low = halves(block_ref[h, c] + top)
            keys_here = k_ref[part(c), :]
            values_here = v_ref[part(c), cols]
            dv_ref[part(c), cols] += weight * (dot(keys_here, high) + dot(keys_here, low))
            dk_one = weight * (dot_nt(values_here, high) + dot_nt(values_here, low))
            dk_acc[part(c), :] += dk_one
            products = keys_here.astype(F32) * dk_one
            key_terms[r] = (
                key_terms[r] + sum_of([dot_nt(ones, x) for x in thirds(products)])[:1]
            )
            if c:
                top = through(h, c) * top

    def store(i, source, target):
        copy = pltpu.make_async_copy(source, target, out_sems.at[i])
        copy.start()
        return copy

    stores = [store(2, dv_ref, dv_out), store(4, dw_ref, dw_out)]

    for c in range(num):
        head_out[c, :STRETCH] = dqt_ref[:, part(c)].T
        head_out[c, STRETCH:] = dk_acc[part(c), :]

    n_chip = n_head // 2
    core, chip = lax.rem(mine, 2), mine // 2
    sibling = chip * 2 + 1 - core
    for x in range(n_chip):
        pltpu.make_async_remote_copy(
            src_ref=head_out.at[2 * x + 1 - core],
            dst_ref=pair_in.at[x],
            send_sem=pair_sems.at[0, x],
            recv_sem=pair_sems.at[1, x],
            device_id={"head": sibling},
        ).start()

    def join(x):
        pltpu.make_async_copy(pair_in.at[x], pair_in.at[x], pair_sems.at[1, x]).wait()
        pair_in[x] = pair_in[x] + head_out[2 * x + core]

    for k in range(1, n_chip):
        x = lax.rem(chip + k, n_chip)
        join(x)
        pltpu.make_async_remote_copy(
            src_ref=pair_in.at[x],
            dst_ref=head_in.at[chip],
            send_sem=sems.at[4],
            recv_sem=sems.at[5],
            device_id={"head": x * 2 + core},
        ).start()
    join(chip)
    head_in[chip] = pair_in[chip]

    got_flow = flow_in.at[pl.ds(0, n_ctx - 1)]
    pltpu.make_async_copy(got_flow, got_flow, sems.at[9]).wait()
    from_here = ones_where(row_at >= lane_at)
    terms = []
    for h in range(heads):
        for c in range(num):
            r = h * num + c
            term = query_terms[r] - key_terms[r]
            for level in range(LOCAL_LEVELS + 1, LOCAL_LEVELS + 1 + bits):
                term = term + w_ref[level, h : h + 1, part(c)] * dw_ref[
                    level, h : h + 1, part(c)
                ]
            terms.append(term)
    terms = jnp.concatenate(terms, axis=0)
    suffix = sum_of([dot(x, from_here) for x in thirds(terms)])
    sums = jnp.broadcast_to(suffix[:, :1], suffix.shape)
    suffix = suffix + sum_of([dot(later, x) for x in thirds(sums)])
    for h in range(heads):
        beyond = sum_of([flow_in[h * per_head + i] for i in range(per_head)])
        beyond = jnp.sum(beyond, axis=1, keepdims=True)
        for c in range(num):
            r = h * num + c
            dg_ref[h : h + 1, part(c)] = suffix[r : r + 1] + beyond
    stores.append(store(3, dg_ref, dg_out))

    for size in range(bits + 1):

        @pl.when(count == size)
        def _(size=size):
            if size:
                sent = out1.at[pl.ds(0, (n_ctx - 1) * size)]
                pltpu.make_async_copy(sent, sent, sems.at[0]).wait()
            sent = out2.at[pl.ds(0, everything - size)]
            pltpu.make_async_copy(sent, sent, sems.at[2]).wait()

    sent = meta_in.at[pl.ds(0, n_ctx - 1)]
    pltpu.make_async_copy(sent, sent, sems.at[6]).wait()
    pltpu.make_async_copy(sent, sent, sems.at[8]).wait()
    sent = s_out.at[pl.ds(0, n_ctx - 1)]
    pltpu.make_async_copy(sent, sent, sems.at[10]).wait()
    pltpu.make_async_copy(sent, sent, sems.at[12]).wait()
    for x in range(n_chip):
        pltpu.make_async_copy(pair_in.at[x], pair_in.at[x], pair_sems.at[0, x]).wait()

    others = head_in.at[pl.ds(0, n_chip - 1)]
    pltpu.make_async_copy(others, others, sems.at[5]).wait()
    pltpu.make_async_copy(others, others, sems.at[4]).wait()
    dq_ref[...] = sum_of([head_in[n, :STRETCH] for n in range(n_chip)])
    dk_ref[...] = sum_of([head_in[n, STRETCH:] for n in range(n_chip)])
    stores.append(store(0, dq_ref, dq_out))
    stores.append(store(1, dk_ref, dk_out))
    for copy in stores:
        copy.wait()


def finish(pieces, *refs):
    half = len(pieces)
    given, results, held = refs[:half], refs[half : 2 * half], refs[2 * half : 3 * half]
    load_sems, store_sems = refs[3 * half :]
    steps = []
    for ref, out, mid, count in zip(given, results, held, pieces):
        size = ref.shape[0] // count
        for at in range(count):
            cut = pl.ds(at * size, size)
            i = len(steps)
            steps.append(
                (
                    pltpu.make_async_copy(ref.at[cut], mid.at[cut], load_sems.at[i]),
                    pltpu.make_async_copy(mid.at[cut], out.at[cut], store_sems.at[i]),
                )
            )
    for load, _ in steps:
        load.start()
    for load, store in steps:
        load.wait()
        store.start()
    for _, store in steps:
        store.wait()


def shards(queries, keys, values, gates, level_weights, segment, cotangent):
    n_ctx, n_head = lax.axis_size("ctx"), lax.axis_size("head")
    heads, tokens = gates.shape
    num = tokens // STRETCH
    bits = n_ctx.bit_length() - 1
    slab_rows = heads * STRETCH // n_ctx
    held = pltpu.VMEM((n_ctx * bits, slab_rows, STRETCH), F32)
    single = pltpu.VMEM((n_ctx, slab_rows, STRETCH), F32)
    turned = pltpu.VMEM((STRETCH, tokens), F32)
    turned_half = pltpu.VMEM((STRETCH, tokens), BF16)

    def chunks(n):
        return pltpu.VMEM((n, 2 * STRETCH, STRETCH), F32)

    anywhere = pl.BlockSpec(memory_space=pl.ANY)
    rows_out = tokens // n_head
    weights = level_weights.transpose(1, 0, 2)
    segments = segment.reshape(num, STRETCH)
    inputs = (queries, keys, values, cotangent, gates, weights, segments)
    results = (
        jax.ShapeDtypeStruct((rows_out, STRETCH), F32),
        jax.ShapeDtypeStruct((rows_out, STRETCH), F32),
        jax.ShapeDtypeStruct(values.shape, F32),
        jax.ShapeDtypeStruct(gates.shape, F32),
        jax.ShapeDtypeStruct(weights.shape, F32),
    )
    raw = pl.pallas_call(
        functools.partial(kernel, n_ctx, n_head),
        out_shape=results,
        in_specs=[anywhere] * 7,
        out_specs=(anywhere,) * 5,
        scratch_shapes=[
            *[pltpu.VMEM(x.shape, x.dtype) for x in (*results, *inputs)],
            turned,
            turned,
            turned_half,
            turned_half,
            pltpu.VMEM((heads, STRETCH, tokens), BF16),
            pltpu.VMEM((heads, num, STRETCH, STRETCH), F32),
            single,
            single,
            held,
            held,
            held,
            held,
            single,
            single,
            turned,
            pltpu.VMEM((tokens, STRETCH), F32),
            pltpu.VMEM((heads, 1, STRETCH), F32),
            pltpu.VMEM((n_ctx, 1, STRETCH), F32),
            pltpu.VMEM((n_ctx, 1, STRETCH), F32),
            pltpu.VMEM((n_ctx, 1, STRETCH), F32),
            chunks(n_head),
            chunks(n_head // 2),
            chunks(n_head // 2),
            pltpu.SemaphoreType.DMA((14,)),
            pltpu.SemaphoreType.DMA((2, n_head // 2)),
            pltpu.SemaphoreType.DMA((7,)),
            pltpu.SemaphoreType.DMA((5,)),
        ],
        compiler_params=pltpu.CompilerParams(
            collective_id=0, has_side_effects=True, vmem_limit_bytes=56 * 2**20
        ),
        name="loglinear_backward",
    )(*inputs)
    pieces = (1, 1, 4, 1, 1)
    *outs, weight_grad = pl.pallas_call(
        functools.partial(finish, pieces),
        out_shape=[jax.ShapeDtypeStruct(x.shape, F32) for x in raw],
        in_specs=[anywhere] * len(raw),
        out_specs=[anywhere] * len(raw),
        scratch_shapes=[
            *[pltpu.VMEM(x.shape, F32) for x in raw],
            pltpu.SemaphoreType.DMA((sum(pieces),)),
            pltpu.SemaphoreType.DMA((sum(pieces),)),
        ],
        name="store_results",
    )(*raw)
    return (*outs, weight_grad.transpose(1, 0, 2))


def solution(mesh):
    return jax.shard_map(
        shards,
        mesh=mesh,
        in_specs=(
            P("ctx", None),
            P("ctx", None),
            P("ctx", "head"),
            P("head", "ctx"),
            P("head", None, "ctx"),
            P("ctx"),
            P("ctx", "head"),
        ),
        out_specs=(
            P(("ctx", "head"), None),
            P(("ctx", "head"), None),
            P("ctx", "head"),
            P("head", "ctx"),
            P("head", None, "ctx"),
        ),
        check_vma=False,
    )
```

```python
import functools

import jax
import jax.numpy as jnp
from jax import lax
from jax.experimental import pallas as pl
from jax.experimental.pallas import tpu as pltpu
from jax.sharding import PartitionSpec as P

STRETCH = 128
LOCAL_LEVELS = 3
F32 = jnp.float32
BF16 = jnp.bfloat16


def halves(x):
    high = x.astype(BF16)
    return high, (x - high.astype(F32)).astype(BF16)


def thirds(x):
    high = x.astype(BF16)
    rest = x - high.astype(F32)
    middle = rest.astype(BF16)
    return high, middle, (rest - middle.astype(F32)).astype(BF16)


def dot(a, b):
    return jnp.dot(a, b, preferred_element_type=F32)


def dot_nt(a, b):
    return lax.dot_general(a, b, (((1,), (1,)), ((), ())), preferred_element_type=F32)


def dot_left(x, exact):
    high, low = halves(x)
    return dot(high, exact) + dot(low, exact)


def dot_right(exact, x):
    high, low = halves(x)
    return dot(exact, high) + dot(exact, low)


def sum_of(terms):
    return functools.reduce(jnp.add, terms)


def ones_where(mask):
    return jnp.where(mask, 1.0, 0.0).astype(BF16)


def part(c):
    return slice(c * STRETCH, (c + 1) * STRETCH)


def pop(number, bits):
    return sum_of([(number >> b) & 1 for b in range(bits)])


def kernel(
    n_ctx,
    n_head,
    q_in,
    k_in,
    v_in,
    c_in,
    g_in,
    w_in,
    s_in,
    dq_out,
    dk_out,
    dv_out,
    dg_out,
    dw_out,
    dq_ref,
    dk_ref,
    dv_ref,
    dg_ref,
    dw_ref,
    q_ref,
    k_ref,
    v_ref,
    c_ref,
    g_ref,
    w_ref,
    s_ref,
    qt_ref,
    kt_ref,
    qtb_ref,
    ktb_ref,
    ctb_ref,
    block_ref,
    s_out,
    s_in_buf,
    out1,
    buf1,
    out2,
    buf2,
    t_out,
    t_in,
    dqt_ref,
    dk_acc,
    product_ref,
    meta_out,
    meta_in,
    flow_out,
    flow_in,
    head_out,
    pair_in,
    head_in,
    sems,
    pair_sems,
    chip_sems,
    in_sems,
    out_sems,
):
    loads = [
        pltpu.make_async_copy(source, target, in_sems.at[i])
        for i, (source, target) in enumerate(
            [
                (g_in, g_ref),
                (s_in, s_ref),
                (k_in, k_ref),
                (v_in, v_ref),
                (q_in, q_ref),
                (c_in, c_ref),
                (w_in, w_ref),
            ]
        )
    ]
    for load in loads:
        load.start()
    heads, tokens = g_ref.shape
    num = tokens // STRETCH
    rows = heads * num
    bits = n_ctx.bit_length() - 1
    slabs = bits
    slab_rows = buf1.shape[1]
    per_head = n_ctx // heads
    me = lax.axis_index("ctx")
    mine = lax.axis_index("head")
    count = pop(me, bits)
    everything = sum(bin(n).count("1") for n in range(n_ctx))

    def partner(k):
        step = (k + 1) // 2
        return lax.rem(jnp.where(lax.rem(k, 2) == 1, me + step, me + n_ctx - step), n_ctx)

    barrier = pltpu.get_barrier_semaphore()

    def greet_ctx(k, _):
        pl.semaphore_signal(barrier, inc=1, device_id={"ctx": lax.rem(me + k, n_ctx)})
        return 0

    def greet_head(k, _):
        pl.semaphore_signal(barrier, inc=1, device_id={"head": lax.rem(mine + k, n_head)})
        return 0

    lax.fori_loop(1, n_ctx, greet_ctx, 0)
    lax.fori_loop(1, n_head, greet_head, 0)

    for load in loads[:2]:
        load.wait()

    gates = jnp.concatenate(
        [g_ref[h : h + 1, part(c)] for h in range(heads) for c in range(num)], axis=0
    )
    seg_one = s_ref[...]
    seg = jnp.concatenate([seg_one] * heads, axis=0)
    row_at = lax.broadcasted_iota(jnp.int32, (STRETCH, STRETCH), 0)
    lane_at = lax.broadcasted_iota(jnp.int32, (STRETCH, STRETCH), 1)
    upto = ones_where(row_at <= lane_at)
    within = sum_of([dot(x, upto) for x in thirds(gates)])
    total = jnp.broadcast_to(within[:, STRETCH - 1 :], within.shape)
    seg_end = jnp.broadcast_to(seg[:, STRETCH - 1 :], seg.shape)
    seg_first = jnp.broadcast_to(seg_one[:, :1], seg_one.shape)[:1]
    ra = lax.broadcasted_iota(jnp.int32, (rows, rows), 0)
    rb = lax.broadcasted_iota(jnp.int32, (rows, rows), 1)
    same_head = (ra // num) == (rb // num)
    earlier = ones_where(same_head & (rb < ra))
    later = ones_where(same_head & (rb > ra))
    before = sum_of([dot(earlier, x) for x in thirds(total)])
    entry = jnp.where(seg == seg_first, jnp.exp(within + before), 0.0)
    key_weight = jnp.where(seg == seg_end, jnp.exp(total - within), 0.0)
    through_exp = jnp.exp(total)

    def end(c):
        return seg_end[c : c + 1]

    def through(h, c):
        r = h * num + c
        return jnp.where(end(c - 1) == end(c), through_exp[r : r + 1], 0.0)

    def local_weight(h, level, c):
        r = h * num + c
        span = 1 << (level - 1)
        base = c // span * span
        shift = before[r : r + 1] - before[h * num + base : h * num + base + 1]
        return jnp.where(
            seg[r : r + 1] == end(base - 1), jnp.exp(within[r : r + 1] + shift), 0.0
        )

    def remote_row(h, k, c):
        picked = jnp.zeros((1, STRETCH), F32)
        for b in range(bits):
            is_it = (((me >> b) & 1) == 1) & (pop(me & ((1 << b) - 1), bits) == k)
            level = LOCAL_LEVELS + 1 + b
            picked = picked + jnp.where(is_it, w_ref[level, h : h + 1, part(c)], 0.0)
        return picked

    def columns(ref, h):
        return ref[:, h * STRETCH : (h + 1) * STRETCH]

    for load in loads[2:]:
        load.wait()

    qt_ref[...] = q_ref[...].astype(F32).T
    kt_ref[...] = k_ref[...].astype(F32).T
    qtb_ref[...] = qt_ref[...].astype(BF16)
    ktb_ref[...] = kt_ref[...].astype(BF16)
    for h in range(heads):
        ctb_ref[h] = columns(c_ref, h).astype(F32).T.astype(BF16)

    for h in range(heads):
        for c in range(num):
            r = h * num + c
            scaled = kt_ref[:, part(c)] * key_weight[r : r + 1]
            block_ref[h, c] = dot_left(scaled, v_ref[part(c), h * STRETCH : (h + 1) * STRETCH])
        state = block_ref[h, 0]
        for c in range(1, num):
            state = through(h, c) * state + block_ref[h, c]
        last = h * num + num - 1
        passes = jnp.where(
            seg_first == end(num - 1), jnp.exp(before[last : last + 1] + total[last : last + 1]), 0.0
        )
        at = lax.broadcasted_iota(jnp.int32, (1, STRETCH), 1)
        meta_out[h] = jnp.where(
            at < 32,
            passes,
            jnp.where(at < 64, seg_first.astype(F32), end(num - 1).astype(F32)),
        )
        for i in range(per_head):
            s_out[h * per_head + i] = state[i * slab_rows : (i + 1) * slab_rows]

    pl.semaphore_wait(barrier, n_ctx + n_head - 2)

    def send_state(k, _):
        to = partner(k)
        pltpu.make_async_remote_copy(
            src_ref=meta_out.at[to // per_head],
            dst_ref=meta_in.at[me],
            send_sem=sems.at[6],
            recv_sem=sems.at[7],
            device_id={"ctx": to},
        ).start()
        pltpu.make_async_remote_copy(
            src_ref=s_out.at[to],
            dst_ref=s_in_buf.at[me],
            send_sem=sems.at[10],
            recv_sem=sems.at[11],
            device_id={"ctx": to},
        ).start()
        return 0

    lax.fori_loop(1, n_ctx, send_state, 0)
    meta_in[me] = meta_out[me // per_head]
    s_in_buf[me] = s_out[me]

    for k in range(bits):

        @pl.when(count > k)
        def _(k=k):
            for h in range(heads):
                scaled = jnp.concatenate(
                    [
                        qt_ref[:, part(c)]
                        * (entry[h * num + c : h * num + c + 1] * remote_row(h, k, c))
                        for c in range(num)
                    ],
                    axis=1,
                )
                grad = dot_left(scaled, columns(c_ref, h))
                for i in range(per_head):
                    out1[(h * per_head + i) * slabs + k] = grad[
                        i * slab_rows : (i + 1) * slab_rows
                    ]

    for size in range(1, bits + 1):

        @pl.when(count == size)
        def _(size=size):
            def send(k, _):
                to = partner(k)
                pltpu.make_async_remote_copy(
                    src_ref=out1.at[pl.ds(to * slabs, size)],
                    dst_ref=buf1.at[pl.ds(me * slabs, size)],
                    send_sem=sems.at[0],
                    recv_sem=sems.at[1],
                    device_id={"ctx": to},
                ).start()
                return 0

            lax.fori_loop(1, n_ctx, send, 0)
            for s in range(size):
                buf1[me * slabs + s] = out1[me * slabs + s]

    got_state = s_in_buf.at[pl.ds(0, n_ctx - 1)]
    pltpu.make_async_copy(got_state, got_state, sems.at[11]).wait()
    got_meta = meta_in.at[pl.ds(0, n_ctx - 1)]
    pltpu.make_async_copy(got_meta, got_meta, sems.at[7]).wait()
    meta_rows = [
        [jnp.broadcast_to(meta_in[n][:, i : i + 1], (1, STRETCH)) for i in (0, 32, 64)]
        for n in range(n_ctx)
    ]
    enter = [None] + [
        jnp.where(meta_rows[n - 1][2] == meta_rows[n][1], 1.0, 0.0) for n in range(1, n_ctx)
    ]
    link = [jnp.zeros_like(meta_rows[0][0])] + [
        meta_rows[n][0] * enter[n] for n in range(1, n_ctx)
    ]

    def rank(n, b):
        return bin(n & ((1 << b) - 1)).count("1")

    blocks = [s_in_buf[n] for n in range(n_ctx)]
    passing = [link]
    factors = {}
    for b in range(bits):
        thru = passing[b]
        for j in range(1, n_ctx >> b, 2):
            lead = None
            for p in range(j << b, (j + 1) << b):
                lead = jnp.ones((1, STRETCH), F32) if lead is None else lead * link[p - 1]
                factors[b, p] = lead * enter[p]
                out2[p * slabs + rank(p, b)] = factors[b, p] * blocks[j - 1]
        half = len(blocks) // 2
        blocks = [thru[2 * j + 1] * blocks[2 * j] + blocks[2 * j + 1] for j in range(half)]
        passing.append([thru[2 * j] * thru[2 * j + 1] for j in range(half)])

    def send_buckets(k, _):
        to = partner(k)
        size_there = pop(to, bits)
        for size in range(1, bits + 1):

            @pl.when(size_there == size)
            def _(size=size):
                pltpu.make_async_remote_copy(
                    src_ref=out2.at[pl.ds(to * slabs, size)],
                    dst_ref=buf2.at[pl.ds(me * slabs, size)],
                    send_sem=sems.at[2],
                    recv_sem=sems.at[3],
                    device_id={"ctx": to},
                ).start()

        return 0

    lax.fori_loop(1, n_ctx, send_buckets, 0)
    for size in range(1, bits + 1):

        @pl.when(count == size)
        def _(size=size):
            for s in range(size):
                buf2[me * slabs + s] = out2[me * slabs + s]

    ones = jnp.ones((8, STRETCH), BF16)
    query_terms = [None] * rows
    for c in range(num):
        seg_row = seg_one[c : c + 1]
        seg_col = jnp.broadcast_to(seg_row.astype(F32), (STRETCH, STRETCH)).T
        allowed = (row_at <= lane_at) & (seg_col == seg_row.astype(F32))
        scores = dot(k_ref[part(c), :], qtb_ref[:, part(c)])
        dk_sum = None
        dq_sum = None
        for h in range(heads):
            r = h * num + c
            cols = slice(h * STRETCH, (h + 1) * STRETCH)
            w_row = within[r : r + 1]
            w_col = jnp.broadcast_to(w_row, (STRETCH, STRETCH)).T
            decay = jnp.where(allowed, jnp.exp(jnp.minimum(w_row - w_col, 0.0)), 0.0)
            pairs = dot(v_ref[part(c), cols], ctb_ref[h, :, part(c)])
            mixed = decay * scores
            weight = w_ref[0, h : h + 1, part(c)]
            d_weight = jnp.sum(mixed * pairs, axis=0, keepdims=True)
            dw_ref[0, h : h + 1, part(c)] = d_weight
            query_terms[r] = weight * d_weight
            dv_ref[part(c), cols] = dot_left(mixed * weight, c_ref[part(c), cols])
            d_scores = decay * pairs * weight
            dk_one = dot_left(d_scores, q_ref[part(c), :])
            dq_one = dot_right(ktb_ref[:, part(c)], d_scores)
            product_ref[h, part(c), :] = k_ref[part(c), :].astype(F32) * dk_one
            dk_sum = dk_one if dk_sum is None else dk_sum + dk_one
            dq_sum = dq_one if dq_sum is None else dq_sum + dq_one
        dk_acc[part(c), :] = dk_sum
        dqt_ref[:, part(c)] = dq_sum

    for size in range(bits + 1):

        @pl.when(count == size)
        def _(size=size):
            got = buf1.at[pl.ds(0, everything - size)]
            pltpu.make_async_copy(got, got, sems.at[1]).wait()

    block_grads = [[None] * (n_ctx >> b) for b in range(bits)]
    flows = [jnp.zeros((slab_rows, STRETCH), F32)] * n_ctx
    for b in range(bits):
        for j in range(1, n_ctx >> b, 2):
            for p in range(j << b, (j + 1) << b):
                slot = p * slabs + rank(p, b)
                grad = buf1[slot]
                flows[p] = flows[p] + out2[slot] * grad
                term = factors[b, p] * grad
                old = block_grads[b][j - 1]
                block_grads[b][j - 1] = term if old is None else old + term
    down = [jnp.zeros((slab_rows, STRETCH), F32)]
    for b in reversed(range(bits)):
        next_down = []
        for j, top in enumerate(down):
            next_down += [block_grads[b][2 * j] + passing[b][2 * j + 1] * top, top]
        down = next_down
    after = jnp.zeros((slab_rows, STRETCH), F32)
    for n in reversed(range(n_ctx)):
        t_out[n] = down[n]
        flow_out[n] = jnp.sum(after, axis=0, keepdims=True)
        after = after + (flows[n] - s_in_buf[n] * down[n])

    def send_grads(k, _):
        to = partner(k)
        pltpu.make_async_remote_copy(
            src_ref=t_out.at[to],
            dst_ref=t_in.at[me],
            send_sem=sems.at[12],
            recv_sem=sems.at[13],
            device_id={"ctx": to},
        ).start()
        pltpu.make_async_remote_copy(
            src_ref=flow_out.at[to],
            dst_ref=flow_in.at[me],
            send_sem=sems.at[8],
            recv_sem=sems.at[9],
            device_id={"ctx": to},
        ).start()
        return 0

    lax.fori_loop(1, n_ctx, send_grads, 0)
    t_in[me] = t_out[me]
    flow_in[me] = flow_out[me]

    state_grads = []
    for h in range(heads):
        cols = slice(h * STRETCH, (h + 1) * STRETCH)
        lower = [block_ref[h, c] for c in range(num)]
        thru = [None] + [through(h, c) for c in range(1, num)]
        thru[0] = jnp.zeros_like(thru[1])
        per_level = []
        thrus = []
        for level in range(1, LOCAL_LEVELS + 1):
            span = 1 << (level - 1)
            grads = [None] * len(lower)
            for j in range(1, len(lower), 2):
                lanes = slice(j * span * STRETCH, (j + 1) * span * STRETCH)
                high, low = halves(lower[j - 1])
                reach = ctb_ref[h, :, lanes]
                got = dot(high, reach) + dot(low, reach)
                scaled = []
                for c in range(j * span, (j + 1) * span):
                    r = h * num + c
                    here = slice((c - j * span) * STRETCH, (c - j * span + 1) * STRETCH)
                    decay = local_weight(h, level, c)
                    q_part = qt_ref[:, part(c)]
                    d_weight = decay * jnp.sum(q_part * got[:, here], axis=0, keepdims=True)
                    weight = w_ref[level, h : h + 1, part(c)]
                    dw_ref[level, h : h + 1, part(c)] = d_weight
                    query_terms[r] = query_terms[r] + weight * d_weight
                    both = weight * decay
                    dqt_ref[:, part(c)] += both * got[:, here]
                    scaled.append(q_part * both)
                scaled = jnp.concatenate(scaled, axis=1) if span > 1 else scaled[0]
                grads[j - 1] = dot_left(scaled, c_ref[lanes, cols])
            for j in range(0, len(lower), 2):
                for c in range(j * span, (j + 1) * span):
                    dw_ref[level, h : h + 1, part(c)] = jnp.zeros((1, STRETCH), F32)
            per_level.append(grads)
            thrus.append(thru)
            lower, thru = (
                [thru[j + 1] * lower[j] + lower[j + 1] for j in range(0, len(lower), 2)],
                [thru[j] * thru[j + 1] for j in range(0, len(lower), 2)],
            )
        down = [None]
        for level in reversed(range(LOCAL_LEVELS)):
            next_down = []
            for j, top in enumerate(down):
                low = per_level[level][2 * j]
                next_down += [low if top is None else low + thrus[level][2 * j + 1] * top, top]
            down = next_down
        for c in range(num - 1):
            block_ref[h, c] = down[c]
        block_ref[h, num - 1] = jnp.zeros((STRETCH, STRETCH), F32)
        state_grads.append(None)

    for size in range(1, bits + 1):

        @pl.when(count == size)
        def _(size=size):
            got = buf2.at[pl.ds(0, (n_ctx - 1) * size)]
            pltpu.make_async_copy(got, got, sems.at[3]).wait()

    def gathered(ref, stride, s, h):
        return jnp.concatenate(
            [ref[(h * per_head + i) * stride + s] for i in range(per_head)], axis=0
        )

    dw_ref[LOCAL_LEVELS + 1 :] = jnp.zeros(
        (dw_ref.shape[0] - LOCAL_LEVELS - 1, heads, tokens), F32
    )
    for k in range(bits):

        @pl.when(count > k)
        def _(k=k):
            for h in range(heads):
                high, low = halves(gathered(buf2, slabs, k, h))
                for c in range(num):
                    reach = ctb_ref[h, :, part(c)]
                    got = dot(high, reach) + dot(low, reach)
                    decay = entry[h * num + c : h * num + c + 1]
                    d_weight = decay * jnp.sum(qt_ref[:, part(c)] * got, axis=0, keepdims=True)
                    dqt_ref[:, part(c)] += (decay * remote_row(h, k, c)) * got
                    for b in range(bits):
                        is_it = (((me >> b) & 1) == 1) & (pop(me & ((1 << b) - 1), bits) == k)
                        level = LOCAL_LEVELS + 1 + b
                        dw_ref[level, h : h + 1, part(c)] += jnp.where(is_it, d_weight, 0.0)

    n_chip = n_head // 2
    core, chip = lax.rem(mine, 2), mine // 2
    sibling = chip * 2 + 1 - core

    def send_pair(kind, x, source):
        pltpu.make_async_remote_copy(
            src_ref=source,
            dst_ref=pair_in.at[kind, x],
            send_sem=pair_sems.at[0, kind, x],
            recv_sem=pair_sems.at[1, kind, x],
            device_id={"head": sibling},
        ).start()

    def join(kind, x):
        arrived = pair_in.at[kind, x]
        pltpu.make_async_copy(arrived, arrived, pair_sems.at[1, kind, x]).wait()
        pair_in[kind, x] = pair_in[kind, x] + head_out[kind, 2 * x + core]

    def send_chips(kind):
        for k in range(1, n_chip):
            x = lax.rem(chip + k, n_chip)
            join(kind, x)
            pltpu.make_async_remote_copy(
                src_ref=pair_in.at[kind, x],
                dst_ref=head_in.at[kind, chip],
                send_sem=chip_sems.at[0, kind],
                recv_sem=chip_sems.at[1, kind],
                device_id={"head": x * 2 + core},
            ).start()
        join(kind, chip)
        head_in[kind, chip] = pair_in[kind, chip]

    def send_if_siblings(kind, c):
        @pl.when(core != c % 2)
        def _():
            send_pair(kind, c // 2, head_out.at[kind, c])

    for c in range(num):
        head_out[0, c] = dqt_ref[:, part(c)].T
        send_if_siblings(0, c)
    send_chips(0)

    got_grads = t_in.at[pl.ds(0, n_ctx - 1)]
    pltpu.make_async_copy(got_grads, got_grads, sems.at[13]).wait()

    tops = [gathered(t_in, 1, 0, h) for h in range(heads)]
    reaches = []
    for h in range(heads):
        to_end = [None] * num
        to_end[num - 1] = jnp.ones((1, STRETCH), F32)
        for c in reversed(range(num - 1)):
            to_end[c] = to_end[c + 1] * through(h, c + 1)
        reaches.append(to_end)
    for c in range(num):
        seg_col = jnp.broadcast_to(seg_one[c : c + 1].astype(F32), (STRETCH, STRETCH)).T
        keys_here = k_ref[part(c), :]
        dk_sum = dk_acc[part(c), :]
        for h in range(heads):
            cols = slice(h * STRETCH, (h + 1) * STRETCH)
            r = h * num + c
            w_col = jnp.broadcast_to(within[r : r + 1], (STRETCH, STRETCH)).T
            weight = jnp.where(
                seg_col == end(c).astype(F32), jnp.exp(total[r : r + 1] - w_col), 0.0
            )
            high, low = halves(block_ref[h, c] + reaches[h][c] * tops[h])
            values_here = v_ref[part(c), cols]
            dv_ref[part(c), cols] += weight * (dot(keys_here, high) + dot(keys_here, low))
            dk_one = weight * (dot_nt(values_here, high) + dot_nt(values_here, low))
            dk_sum = dk_sum + dk_one
            product_ref[h, part(c), :] += keys_here.astype(F32) * dk_one
        head_out[1, c] = dk_sum
        send_if_siblings(1, c)
    send_chips(1)

    def store(i, source, target):
        copy = pltpu.make_async_copy(source, target, out_sems.at[i])
        copy.start()
        return copy

    stores = [store(2, dv_ref, dv_out), store(4, dw_ref, dw_out)]

    got_flow = flow_in.at[pl.ds(0, n_ctx - 1)]
    pltpu.make_async_copy(got_flow, got_flow, sems.at[9]).wait()
    from_here = ones_where(row_at >= lane_at)
    terms = []
    for h in range(heads):
        for c in range(num):
            r = h * num + c
            sums = sum_of([dot_nt(ones, x) for x in thirds(product_ref[h, part(c), :])])
            term = query_terms[r] - sums[:1]
            for level in range(LOCAL_LEVELS + 1, LOCAL_LEVELS + 1 + bits):
                term = term + w_ref[level, h : h + 1, part(c)] * dw_ref[
                    level, h : h + 1, part(c)
                ]
            terms.append(term)
    terms = jnp.concatenate(terms, axis=0)
    suffix = sum_of([dot(x, from_here) for x in thirds(terms)])
    sums = jnp.broadcast_to(suffix[:, :1], suffix.shape)
    suffix = suffix + sum_of([dot(later, x) for x in thirds(sums)])
    for h in range(heads):
        beyond = sum_of([flow_in[h * per_head + i] for i in range(per_head)])
        beyond = jnp.sum(beyond, axis=1, keepdims=True)
        for c in range(num):
            r = h * num + c
            dg_ref[h : h + 1, part(c)] = suffix[r : r + 1] + beyond
    stores.append(store(3, dg_ref, dg_out))

    for size in range(bits + 1):

        @pl.when(count == size)
        def _(size=size):
            if size:
                sent = out1.at[pl.ds(0, (n_ctx - 1) * size)]
                pltpu.make_async_copy(sent, sent, sems.at[0]).wait()
            sent = out2.at[pl.ds(0, everything - size)]
            pltpu.make_async_copy(sent, sent, sems.at[2]).wait()

    sent = meta_in.at[pl.ds(0, n_ctx - 1)]
    pltpu.make_async_copy(sent, sent, sems.at[6]).wait()
    pltpu.make_async_copy(sent, sent, sems.at[8]).wait()
    sent = s_out.at[pl.ds(0, n_ctx - 1)]
    pltpu.make_async_copy(sent, sent, sems.at[10]).wait()
    pltpu.make_async_copy(sent, sent, sems.at[12]).wait()
    others = head_in.at[0, pl.ds(0, n_chip - 1)]
    for kind, result in enumerate((dq_ref, dk_ref)):
        for x in range(n_chip):
            sent = pair_in.at[kind, x]
            pltpu.make_async_copy(sent, sent, pair_sems.at[0, kind, x]).wait()
        pltpu.make_async_copy(others, others, chip_sems.at[1, kind]).wait()
        pltpu.make_async_copy(others, others, chip_sems.at[0, kind]).wait()
        result[...] = sum_of([head_in[kind, n] for n in range(n_chip)])
    stores.append(store(0, dq_ref, dq_out))
    stores.append(store(1, dk_ref, dk_out))
    for copy in stores:
        copy.wait()


def finish(pieces, *refs):
    half = len(pieces)
    given, results, held = refs[:half], refs[half : 2 * half], refs[2 * half : 3 * half]
    load_sems, store_sems = refs[3 * half :]
    steps = []
    for ref, out, mid, count in zip(given, results, held, pieces):
        size = ref.shape[0] // count
        for at in range(count):
            cut = pl.ds(at * size, size)
            i = len(steps)
            steps.append(
                (
                    pltpu.make_async_copy(ref.at[cut], mid.at[cut], load_sems.at[i]),
                    pltpu.make_async_copy(mid.at[cut], out.at[cut], store_sems.at[i]),
                )
            )
    for load, _ in steps:
        load.start()
    for load, store in steps:
        load.wait()
        store.start()
    for _, store in steps:
        store.wait()


def shards(queries, keys, values, gates, level_weights, segment, cotangent):
    n_ctx, n_head = lax.axis_size("ctx"), lax.axis_size("head")
    heads, tokens = gates.shape
    num = tokens // STRETCH
    bits = n_ctx.bit_length() - 1
    slab_rows = heads * STRETCH // n_ctx
    held = pltpu.VMEM((n_ctx * bits, slab_rows, STRETCH), F32)
    single = pltpu.VMEM((n_ctx, slab_rows, STRETCH), F32)
    turned = pltpu.VMEM((STRETCH, tokens), F32)
    turned_half = pltpu.VMEM((STRETCH, tokens), BF16)

    def chunks(n):
        return pltpu.VMEM((2, n, STRETCH, STRETCH), F32)

    anywhere = pl.BlockSpec(memory_space=pl.ANY)
    rows_out = tokens // n_head
    weights = level_weights.transpose(1, 0, 2)
    segments = segment.reshape(num, STRETCH)
    inputs = (queries, keys, values, cotangent, gates, weights, segments)
    results = (
        jax.ShapeDtypeStruct((rows_out, STRETCH), F32),
        jax.ShapeDtypeStruct((rows_out, STRETCH), F32),
        jax.ShapeDtypeStruct(values.shape, F32),
        jax.ShapeDtypeStruct(gates.shape, F32),
        jax.ShapeDtypeStruct(weights.shape, F32),
    )
    raw = pl.pallas_call(
        functools.partial(kernel, n_ctx, n_head),
        out_shape=results,
        in_specs=[anywhere] * 7,
        out_specs=(anywhere,) * 5,
        scratch_shapes=[
            *[pltpu.VMEM(x.shape, x.dtype) for x in (*results, *inputs)],
            turned,
            turned,
            turned_half,
            turned_half,
            pltpu.VMEM((heads, STRETCH, tokens), BF16),
            pltpu.VMEM((heads, num, STRETCH, STRETCH), F32),
            single,
            single,
            held,
            held,
            held,
            held,
            single,
            single,
            turned,
            pltpu.VMEM((tokens, STRETCH), F32),
            pltpu.VMEM((heads, tokens, STRETCH), F32),
            pltpu.VMEM((heads, 1, STRETCH), F32),
            pltpu.VMEM((n_ctx, 1, STRETCH), F32),
            pltpu.VMEM((n_ctx, 1, STRETCH), F32),
            pltpu.VMEM((n_ctx, 1, STRETCH), F32),
            chunks(n_head),
            chunks(n_head // 2),
            chunks(n_head // 2),
            pltpu.SemaphoreType.DMA((14,)),
            pltpu.SemaphoreType.DMA((2, 2, n_head // 2)),
            pltpu.SemaphoreType.DMA((2, 2)),
            pltpu.SemaphoreType.DMA((7,)),
            pltpu.SemaphoreType.DMA((5,)),
        ],
        compiler_params=pltpu.CompilerParams(
            collective_id=0, has_side_effects=True, vmem_limit_bytes=56 * 2**20
        ),
        name="loglinear_backward",
    )(*inputs)
    pieces = (1, 1, 4, 1, 1)
    *outs, weight_grad = pl.pallas_call(
        functools.partial(finish, pieces),
        out_shape=[jax.ShapeDtypeStruct(x.shape, F32) for x in raw],
        in_specs=[anywhere] * len(raw),
        out_specs=[anywhere] * len(raw),
        scratch_shapes=[
            *[pltpu.VMEM(x.shape, F32) for x in raw],
            pltpu.SemaphoreType.DMA((sum(pieces),)),
            pltpu.SemaphoreType.DMA((sum(pieces),)),
        ],
        name="store_results",
    )(*raw)
    return (*outs, weight_grad.transpose(1, 0, 2))


def solution(mesh):
    return jax.shard_map(
        shards,
        mesh=mesh,
        in_specs=(
            P("ctx", None),
            P("ctx", None),
            P("ctx", "head"),
            P("head", "ctx"),
            P("head", None, "ctx"),
            P("ctx"),
            P("ctx", "head"),
        ),
        out_specs=(
            P(("ctx", "head"), None),
            P(("ctx", "head"), None),
            P("ctx", "head"),
            P("head", "ctx"),
            P("head", None, "ctx"),
        ),
        check_vma=False,
    )
```

```python
import functools

import jax
import jax.numpy as jnp
from jax import lax
from jax.experimental import pallas as pl
from jax.experimental.pallas import tpu as pltpu
from jax.sharding import PartitionSpec as P

STRETCH = 128
LOCAL_LEVELS = 3
F32 = jnp.float32
BF16 = jnp.bfloat16


def halves(x):
    high = x.astype(BF16)
    return high, (x - high.astype(F32)).astype(BF16)


def thirds(x):
    high = x.astype(BF16)
    rest = x - high.astype(F32)
    middle = rest.astype(BF16)
    return high, middle, (rest - middle.astype(F32)).astype(BF16)


def dot(a, b):
    return jnp.dot(a, b, preferred_element_type=F32)


def dot_nt(a, b):
    return lax.dot_general(a, b, (((1,), (1,)), ((), ())), preferred_element_type=F32)


def dot_left(x, exact):
    high, low = halves(x)
    return dot(high, exact) + dot(low, exact)


def dot_right(exact, x):
    high, low = halves(x)
    return dot(exact, high) + dot(exact, low)


def sum_of(terms):
    return functools.reduce(jnp.add, terms)


def ones_where(mask):
    return jnp.where(mask, 1.0, 0.0).astype(BF16)


def part(c):
    return slice(c * STRETCH, (c + 1) * STRETCH)


def pop(number, bits):
    return sum_of([(number >> b) & 1 for b in range(bits)])


def kernel(
    n_ctx,
    n_head,
    q_in,
    k_in,
    v_in,
    c_in,
    g_in,
    w_in,
    s_in,
    dq_out,
    dk_out,
    dv_out,
    dg_out,
    dw_out,
    dq_ref,
    dk_ref,
    dv_ref,
    dg_ref,
    dw_ref,
    q_ref,
    k_ref,
    v_ref,
    c_ref,
    g_ref,
    w_ref,
    s_ref,
    qt_ref,
    kt_ref,
    qtb_ref,
    ktb_ref,
    ctb_ref,
    block_ref,
    s_out,
    s_in_buf,
    out1,
    buf1,
    out2,
    buf2,
    t_out,
    t_in,
    dqt_ref,
    dk_acc,
    product_ref,
    row_ref,
    meta_out,
    meta_in,
    flow_out,
    flow_in,
    head_out,
    pair_in,
    head_in,
    sems,
    pair_sems,
    chip_sems,
    in_sems,
    out_sems,
):
    loads = [
        pltpu.make_async_copy(source, target, in_sems.at[i])
        for i, (source, target) in enumerate(
            [
                (g_in, g_ref),
                (s_in, s_ref),
                (k_in, k_ref),
                (v_in, v_ref),
                (q_in, q_ref),
                (c_in, c_ref),
                (w_in, w_ref),
            ]
        )
    ]
    for load in loads:
        load.start()
    heads, tokens = g_ref.shape
    num = tokens // STRETCH
    rows = heads * num
    bits = n_ctx.bit_length() - 1
    slabs = bits
    slab_rows = buf1.shape[1]
    per_head = n_ctx // heads
    me = lax.axis_index("ctx")
    mine = lax.axis_index("head")
    count = pop(me, bits)
    everything = sum(bin(n).count("1") for n in range(n_ctx))

    def partner(k):
        step = (k + 1) // 2
        return lax.rem(jnp.where(lax.rem(k, 2) == 1, me + step, me + n_ctx - step), n_ctx)

    barrier = pltpu.get_barrier_semaphore()

    def greet_ctx(k, _):
        pl.semaphore_signal(barrier, inc=1, device_id={"ctx": lax.rem(me + k, n_ctx)})
        return 0

    def greet_head(k, _):
        pl.semaphore_signal(barrier, inc=1, device_id={"head": lax.rem(mine + k, n_head)})
        return 0

    lax.fori_loop(1, n_ctx, greet_ctx, 0)
    lax.fori_loop(1, n_head, greet_head, 0)

    for load in loads[:2]:
        load.wait()

    gates = jnp.concatenate(
        [g_ref[h : h + 1, part(c)] for h in range(heads) for c in range(num)], axis=0
    )
    seg_one = s_ref[...]
    seg = jnp.concatenate([seg_one] * heads, axis=0)
    row_at = lax.broadcasted_iota(jnp.int32, (STRETCH, STRETCH), 0)
    lane_at = lax.broadcasted_iota(jnp.int32, (STRETCH, STRETCH), 1)
    upto = ones_where(row_at <= lane_at)
    within = sum_of([dot(x, upto) for x in thirds(gates)])
    total = jnp.broadcast_to(within[:, STRETCH - 1 :], within.shape)
    seg_end = jnp.broadcast_to(seg[:, STRETCH - 1 :], seg.shape)
    seg_first = jnp.broadcast_to(seg_one[:, :1], seg_one.shape)[:1]
    ra = lax.broadcasted_iota(jnp.int32, (rows, rows), 0)
    rb = lax.broadcasted_iota(jnp.int32, (rows, rows), 1)
    same_head = (ra // num) == (rb // num)
    earlier = ones_where(same_head & (rb < ra))
    later = ones_where(same_head & (rb > ra))
    before = sum_of([dot(earlier, x) for x in thirds(total)])
    entry = jnp.where(seg == seg_first, jnp.exp(within + before), 0.0)
    key_weight = jnp.where(seg == seg_end, jnp.exp(total - within), 0.0)
    through_exp = jnp.exp(total)

    def end(c):
        return seg_end[c : c + 1]

    def through(h, c):
        r = h * num + c
        return jnp.where(end(c - 1) == end(c), through_exp[r : r + 1], 0.0)

    def local_weight(h, level, c):
        r = h * num + c
        span = 1 << (level - 1)
        base = c // span * span
        shift = before[r : r + 1] - before[h * num + base : h * num + base + 1]
        return jnp.where(
            seg[r : r + 1] == end(base - 1), jnp.exp(within[r : r + 1] + shift), 0.0
        )

    def remote_row(h, k, c):
        picked = jnp.zeros((1, STRETCH), F32)
        for b in range(bits):
            is_it = (((me >> b) & 1) == 1) & (pop(me & ((1 << b) - 1), bits) == k)
            level = LOCAL_LEVELS + 1 + b
            picked = picked + jnp.where(is_it, w_ref[level, h : h + 1, part(c)], 0.0)
        return picked

    def columns(ref, h):
        return ref[:, h * STRETCH : (h + 1) * STRETCH]

    for load in loads[2:4]:
        load.wait()
    kt_ref[...] = k_ref[...].astype(F32).T

    for h in range(heads):
        for c in range(num):
            r = h * num + c
            scaled = kt_ref[:, part(c)] * key_weight[r : r + 1]
            block_ref[h, c] = dot_left(scaled, v_ref[part(c), h * STRETCH : (h + 1) * STRETCH])
        state = block_ref[h, 0]
        for c in range(1, num):
            state = through(h, c) * state + block_ref[h, c]
        last = h * num + num - 1
        passes = jnp.where(
            seg_first == end(num - 1), jnp.exp(before[last : last + 1] + total[last : last + 1]), 0.0
        )
        at = lax.broadcasted_iota(jnp.int32, (1, STRETCH), 1)
        meta_out[h] = jnp.where(
            at < 32,
            passes,
            jnp.where(at < 64, seg_first.astype(F32), end(num - 1).astype(F32)),
        )
        for i in range(per_head):
            s_out[h * per_head + i] = state[i * slab_rows : (i + 1) * slab_rows]

    pl.semaphore_wait(barrier, n_ctx + n_head - 2)

    def send_state(k, _):
        to = partner(k)
        pltpu.make_async_remote_copy(
            src_ref=meta_out.at[to // per_head],
            dst_ref=meta_in.at[me],
            send_sem=sems.at[6],
            recv_sem=sems.at[7],
            device_id={"ctx": to},
        ).start()
        pltpu.make_async_remote_copy(
            src_ref=s_out.at[to],
            dst_ref=s_in_buf.at[me],
            send_sem=sems.at[10],
            recv_sem=sems.at[11],
            device_id={"ctx": to},
        ).start()
        return 0

    lax.fori_loop(1, n_ctx, send_state, 0)
    meta_in[me] = meta_out[me // per_head]
    s_in_buf[me] = s_out[me]

    for load in loads[4:]:
        load.wait()
    qt_ref[...] = q_ref[...].astype(F32).T

    for k in range(bits):

        @pl.when(count > k)
        def _(k=k):
            for h in range(heads):
                scaled = jnp.concatenate(
                    [
                        qt_ref[:, part(c)]
                        * (entry[h * num + c : h * num + c + 1] * remote_row(h, k, c))
                        for c in range(num)
                    ],
                    axis=1,
                )
                grad = dot_left(scaled, columns(c_ref, h))
                for i in range(per_head):
                    out1[(h * per_head + i) * slabs + k] = grad[
                        i * slab_rows : (i + 1) * slab_rows
                    ]

    for size in range(1, bits + 1):

        @pl.when(count == size)
        def _(size=size):
            def send(k, _):
                to = partner(k)
                pltpu.make_async_remote_copy(
                    src_ref=out1.at[pl.ds(to * slabs, size)],
                    dst_ref=buf1.at[pl.ds(me * slabs, size)],
                    send_sem=sems.at[0],
                    recv_sem=sems.at[1],
                    device_id={"ctx": to},
                ).start()
                return 0

            lax.fori_loop(1, n_ctx, send, 0)
            for s in range(size):
                buf1[me * slabs + s] = out1[me * slabs + s]

    qtb_ref[...] = qt_ref[...].astype(BF16)
    ktb_ref[...] = kt_ref[...].astype(BF16)
    for h in range(heads):
        ctb_ref[h] = columns(c_ref, h).astype(F32).T.astype(BF16)

    got_state = s_in_buf.at[pl.ds(0, n_ctx - 1)]
    pltpu.make_async_copy(got_state, got_state, sems.at[11]).wait()
    got_meta = meta_in.at[pl.ds(0, n_ctx - 1)]
    pltpu.make_async_copy(got_meta, got_meta, sems.at[7]).wait()
    meta_rows = [
        [jnp.broadcast_to(meta_in[n][:, i : i + 1], (1, STRETCH)) for i in (0, 32, 64)]
        for n in range(n_ctx)
    ]
    enter = [None] + [
        jnp.where(meta_rows[n - 1][2] == meta_rows[n][1], 1.0, 0.0) for n in range(1, n_ctx)
    ]
    link = [jnp.zeros_like(meta_rows[0][0])] + [
        meta_rows[n][0] * enter[n] for n in range(1, n_ctx)
    ]

    def rank(n, b):
        return bin(n & ((1 << b) - 1)).count("1")

    blocks = [s_in_buf[n] for n in range(n_ctx)]
    passing = [link]
    factors = {}
    for b in range(bits):
        thru = passing[b]
        for j in range(1, n_ctx >> b, 2):
            lead = None
            for p in range(j << b, (j + 1) << b):
                lead = jnp.ones((1, STRETCH), F32) if lead is None else lead * link[p - 1]
                factors[b, p] = lead * enter[p]
                out2[p * slabs + rank(p, b)] = factors[b, p] * blocks[j - 1]
        half = len(blocks) // 2
        blocks = [thru[2 * j + 1] * blocks[2 * j] + blocks[2 * j + 1] for j in range(half)]
        passing.append([thru[2 * j] * thru[2 * j + 1] for j in range(half)])

    def send_buckets(k, _):
        to = partner(k)
        size_there = pop(to, bits)
        for size in range(1, bits + 1):

            @pl.when(size_there == size)
            def _(size=size):
                pltpu.make_async_remote_copy(
                    src_ref=out2.at[pl.ds(to * slabs, size)],
                    dst_ref=buf2.at[pl.ds(me * slabs, size)],
                    send_sem=sems.at[2],
                    recv_sem=sems.at[3],
                    device_id={"ctx": to},
                ).start()

        return 0

    lax.fori_loop(1, n_ctx, send_buckets, 0)
    for size in range(1, bits + 1):

        @pl.when(count == size)
        def _(size=size):
            for s in range(size):
                buf2[me * slabs + s] = out2[me * slabs + s]

    ones = jnp.ones((8, STRETCH), BF16)
    query_terms = [None] * rows
    for c in range(num):
        seg_row = seg_one[c : c + 1]
        seg_col = jnp.broadcast_to(seg_row.astype(F32), (STRETCH, STRETCH)).T
        allowed = (row_at <= lane_at) & (seg_col == seg_row.astype(F32))
        scores = dot(k_ref[part(c), :], qtb_ref[:, part(c)])
        dk_sum = None
        dq_sum = None
        for h in range(heads):
            r = h * num + c
            cols = slice(h * STRETCH, (h + 1) * STRETCH)
            w_row = within[r : r + 1]
            w_col = jnp.broadcast_to(w_row, (STRETCH, STRETCH)).T
            decay = jnp.where(allowed, jnp.exp(jnp.minimum(w_row - w_col, 0.0)), 0.0)
            pairs = dot(v_ref[part(c), cols], ctb_ref[h, :, part(c)])
            mixed = decay * scores
            weight = w_ref[0, h : h + 1, part(c)]
            d_weight = jnp.sum(mixed * pairs, axis=0, keepdims=True)
            dw_ref[0, h : h + 1, part(c)] = d_weight
            query_terms[r] = weight * d_weight
            dv_ref[part(c), cols] = dot_left(mixed * weight, c_ref[part(c), cols])
            d_scores = decay * pairs * weight
            dk_one = dot_left(d_scores, q_ref[part(c), :])
            dq_one = dot_right(ktb_ref[:, part(c)], d_scores)
            product_ref[h, part(c), :] = k_ref[part(c), :].astype(F32) * dk_one
            dk_sum = dk_one if dk_sum is None else dk_sum + dk_one
            dq_sum = dq_one if dq_sum is None else dq_sum + dq_one
        dk_acc[part(c), :] = dk_sum
        dqt_ref[:, part(c)] = dq_sum

    for size in range(bits + 1):

        @pl.when(count == size)
        def _(size=size):
            got = buf1.at[pl.ds(0, everything - size)]
            pltpu.make_async_copy(got, got, sems.at[1]).wait()

    block_grads = [[None] * (n_ctx >> b) for b in range(bits)]
    for b in range(bits):
        for j in range(1, n_ctx >> b, 2):
            block_grads[b][j - 1] = sum_of(
                [
                    factors[b, p] * buf1[p * slabs + rank(p, b)]
                    for p in range(j << b, (j + 1) << b)
                ]
            )
    down = [jnp.zeros((slab_rows, STRETCH), F32)]
    for b in reversed(range(bits)):
        next_down = []
        for j, top in enumerate(down):
            next_down += [block_grads[b][2 * j] + passing[b][2 * j + 1] * top, top]
        down = next_down
    for n in range(n_ctx):
        t_out[n] = down[n]

    def send_grads(k, _):
        to = partner(k)
        pltpu.make_async_remote_copy(
            src_ref=t_out.at[to],
            dst_ref=t_in.at[me],
            send_sem=sems.at[12],
            recv_sem=sems.at[13],
            device_id={"ctx": to},
        ).start()
        return 0

    lax.fori_loop(1, n_ctx, send_grads, 0)
    t_in[me] = t_out[me]

    after = jnp.zeros((slab_rows, STRETCH), F32)
    for n in reversed(range(n_ctx)):
        flow_out[n] = jnp.sum(after, axis=0, keepdims=True)
        after = after - s_in_buf[n] * t_out[n]
        for slot in range(n * slabs, n * slabs + bin(n).count("1")):
            after = after + out2[slot] * buf1[slot]

    def send_flows(k, _):
        to = partner(k)
        pltpu.make_async_remote_copy(
            src_ref=flow_out.at[to],
            dst_ref=flow_in.at[me],
            send_sem=sems.at[8],
            recv_sem=sems.at[9],
            device_id={"ctx": to},
        ).start()
        return 0

    lax.fori_loop(1, n_ctx, send_flows, 0)
    flow_in[me] = flow_out[me]

    state_grads = []
    for h in range(heads):
        cols = slice(h * STRETCH, (h + 1) * STRETCH)
        lower = [block_ref[h, c] for c in range(num)]
        thru = [None] + [through(h, c) for c in range(1, num)]
        thru[0] = jnp.zeros_like(thru[1])
        per_level = []
        thrus = []
        for level in range(1, LOCAL_LEVELS + 1):
            span = 1 << (level - 1)
            grads = [None] * len(lower)
            for j in range(1, len(lower), 2):
                lanes = slice(j * span * STRETCH, (j + 1) * span * STRETCH)
                high, low = halves(lower[j - 1])
                reach = ctb_ref[h, :, lanes]
                got = dot(high, reach) + dot(low, reach)
                scaled = []
                for c in range(j * span, (j + 1) * span):
                    r = h * num + c
                    here = slice((c - j * span) * STRETCH, (c - j * span + 1) * STRETCH)
                    decay = local_weight(h, level, c)
                    q_part = qt_ref[:, part(c)]
                    d_weight = decay * jnp.sum(q_part * got[:, here], axis=0, keepdims=True)
                    weight = w_ref[level, h : h + 1, part(c)]
                    dw_ref[level, h : h + 1, part(c)] = d_weight
                    query_terms[r] = query_terms[r] + weight * d_weight
                    both = weight * decay
                    dqt_ref[:, part(c)] += both * got[:, here]
                    scaled.append(q_part * both)
                scaled = jnp.concatenate(scaled, axis=1) if span > 1 else scaled[0]
                grads[j - 1] = dot_left(scaled, c_ref[lanes, cols])
            for j in range(0, len(lower), 2):
                for c in range(j * span, (j + 1) * span):
                    dw_ref[level, h : h + 1, part(c)] = jnp.zeros((1, STRETCH), F32)
            per_level.append(grads)
            thrus.append(thru)
            lower, thru = (
                [thru[j + 1] * lower[j] + lower[j + 1] for j in range(0, len(lower), 2)],
                [thru[j] * thru[j + 1] for j in range(0, len(lower), 2)],
            )
        down = [None]
        for level in reversed(range(LOCAL_LEVELS)):
            next_down = []
            for j, top in enumerate(down):
                low = per_level[level][2 * j]
                next_down += [low if top is None else low + thrus[level][2 * j + 1] * top, top]
            down = next_down
        for c in range(num - 1):
            block_ref[h, c] = down[c]
        block_ref[h, num - 1] = jnp.zeros((STRETCH, STRETCH), F32)
        state_grads.append(None)

    for size in range(1, bits + 1):

        @pl.when(count == size)
        def _(size=size):
            got = buf2.at[pl.ds(0, (n_ctx - 1) * size)]
            pltpu.make_async_copy(got, got, sems.at[3]).wait()

    def gathered(ref, stride, s, h):
        return jnp.concatenate(
            [ref[(h * per_head + i) * stride + s] for i in range(per_head)], axis=0
        )

    dw_ref[LOCAL_LEVELS + 1 :] = jnp.zeros(
        (dw_ref.shape[0] - LOCAL_LEVELS - 1, heads, tokens), F32
    )
    for k in range(bits):

        @pl.when(count > k)
        def _(k=k):
            for h in range(heads):
                high, low = halves(gathered(buf2, slabs, k, h))
                for c in range(num):
                    reach = ctb_ref[h, :, part(c)]
                    got = dot(high, reach) + dot(low, reach)
                    decay = entry[h * num + c : h * num + c + 1]
                    d_weight = decay * jnp.sum(qt_ref[:, part(c)] * got, axis=0, keepdims=True)
                    dqt_ref[:, part(c)] += (decay * remote_row(h, k, c)) * got
                    for b in range(bits):
                        is_it = (((me >> b) & 1) == 1) & (pop(me & ((1 << b) - 1), bits) == k)
                        level = LOCAL_LEVELS + 1 + b
                        dw_ref[level, h : h + 1, part(c)] += jnp.where(is_it, d_weight, 0.0)

    n_chip = n_head // 2
    core, chip = lax.rem(mine, 2), mine // 2
    sibling = chip * 2 + 1 - core

    def send_pair(kind, x, source):
        pltpu.make_async_remote_copy(
            src_ref=source,
            dst_ref=pair_in.at[kind, x],
            send_sem=pair_sems.at[0, kind, x],
            recv_sem=pair_sems.at[1, kind, x],
            device_id={"head": sibling},
        ).start()

    def join(kind, x):
        arrived = pair_in.at[kind, x]
        pltpu.make_async_copy(arrived, arrived, pair_sems.at[1, kind, x]).wait()
        pair_in[kind, x] = pair_in[kind, x] + head_out[kind, 2 * x + core]

    def send_chip(kind, x):
        join(kind, x)
        pltpu.make_async_remote_copy(
            src_ref=pair_in.at[kind, x],
            dst_ref=head_in.at[kind, chip],
            send_sem=chip_sems.at[0, kind],
            recv_sem=chip_sems.at[1, kind],
            device_id={"head": x * 2 + core},
        ).start()

    def send_if_siblings(kind, c):
        @pl.when(core != c % 2)
        def _():
            send_pair(kind, c // 2, head_out.at[kind, c])

    for c in range(num):
        head_out[0, c] = dqt_ref[:, part(c)].T
        send_if_siblings(0, c)
    for k in range(1, n_chip):
        send_chip(0, lax.rem(chip + k, n_chip))
    join(0, chip)
    head_in[0, chip] = pair_in[0, chip]

    for h in range(heads):
        reach = jnp.ones((1, STRETCH), F32)
        for c in reversed(range(num)):
            r = h * num + c
            row_ref[0, r] = within[r : r + 1]
            row_ref[1, r] = total[r : r + 1]
            row_ref[2, r] = end(c).astype(F32)
            row_ref[3, r] = seg_one[c : c + 1].astype(F32)
            row_ref[4, r] = reach
            if c:
                reach = reach * through(h, c)

    got_grads = t_in.at[pl.ds(0, n_ctx - 1)]
    pltpu.make_async_copy(got_grads, got_grads, sems.at[13]).wait()
    tops = [gathered(t_in, 1, 0, h) for h in range(heads)]

    def finish_keys(c):
        here = pl.ds(pl.multiple_of(c * STRETCH, STRETCH), STRETCH)
        seg_col = jnp.broadcast_to(row_ref[3, c], (STRETCH, STRETCH)).T
        keys_here = k_ref[here, :]
        dk_sum = dk_acc[here, :]
        for h in range(heads):
            cols = slice(h * STRETCH, (h + 1) * STRETCH)
            r = h * num + c
            w_col = jnp.broadcast_to(row_ref[0, r], (STRETCH, STRETCH)).T
            weight = jnp.where(
                seg_col == row_ref[2, r], jnp.exp(row_ref[1, r] - w_col), 0.0
            )
            high, low = halves(block_ref[h, c] + row_ref[4, r] * tops[h])
            values_here = v_ref[here, cols]
            dv_ref[here, cols] += weight * (dot(keys_here, high) + dot(keys_here, low))
            dk_one = weight * (dot_nt(values_here, high) + dot_nt(values_here, low))
            dk_sum = dk_sum + dk_one
            product_ref[h, here, :] += keys_here.astype(F32) * dk_one
        head_out[1, c] = dk_sum

    chip_order = [lax.rem(chip + k, n_chip) for k in range(1, n_chip + 1)]
    for k, x in enumerate(chip_order):
        finish_keys(2 * x + 1 - core)
        send_pair(1, x, head_out.at[1, 2 * x + 1 - core])
        finish_keys(2 * x + core)
        if k:
            send_chip(1, chip_order[k - 1])
    join(1, chip)
    head_in[1, chip] = pair_in[1, chip]

    def store(i, source, target):
        copy = pltpu.make_async_copy(source, target, out_sems.at[i])
        copy.start()
        return copy

    stores = [store(2, dv_ref, dv_out), store(4, dw_ref, dw_out)]

    got_flow = flow_in.at[pl.ds(0, n_ctx - 1)]
    pltpu.make_async_copy(got_flow, got_flow, sems.at[9]).wait()
    from_here = ones_where(row_at >= lane_at)
    terms = []
    for h in range(heads):
        for c in range(num):
            r = h * num + c
            sums = sum_of([dot_nt(ones, x) for x in thirds(product_ref[h, part(c), :])])
            term = query_terms[r] - sums[:1]
            for level in range(LOCAL_LEVELS + 1, LOCAL_LEVELS + 1 + bits):
                term = term + w_ref[level, h : h + 1, part(c)] * dw_ref[
                    level, h : h + 1, part(c)
                ]
            terms.append(term)
    terms = jnp.concatenate(terms, axis=0)
    suffix = sum_of([dot(x, from_here) for x in thirds(terms)])
    sums = jnp.broadcast_to(suffix[:, :1], suffix.shape)
    suffix = suffix + sum_of([dot(later, x) for x in thirds(sums)])
    for h in range(heads):
        beyond = sum_of([flow_in[h * per_head + i] for i in range(per_head)])
        beyond = jnp.sum(beyond, axis=1, keepdims=True)
        for c in range(num):
            r = h * num + c
            dg_ref[h : h + 1, part(c)] = suffix[r : r + 1] + beyond
    stores.append(store(3, dg_ref, dg_out))

    for size in range(bits + 1):

        @pl.when(count == size)
        def _(size=size):
            if size:
                sent = out1.at[pl.ds(0, (n_ctx - 1) * size)]
                pltpu.make_async_copy(sent, sent, sems.at[0]).wait()
            sent = out2.at[pl.ds(0, everything - size)]
            pltpu.make_async_copy(sent, sent, sems.at[2]).wait()

    sent = meta_in.at[pl.ds(0, n_ctx - 1)]
    pltpu.make_async_copy(sent, sent, sems.at[6]).wait()
    pltpu.make_async_copy(sent, sent, sems.at[8]).wait()
    sent = s_out.at[pl.ds(0, n_ctx - 1)]
    pltpu.make_async_copy(sent, sent, sems.at[10]).wait()
    pltpu.make_async_copy(sent, sent, sems.at[12]).wait()
    others = head_in.at[0, pl.ds(0, n_chip - 1)]
    for kind, result in enumerate((dq_ref, dk_ref)):
        for x in range(n_chip):
            sent = pair_in.at[kind, x]
            pltpu.make_async_copy(sent, sent, pair_sems.at[0, kind, x]).wait()
        pltpu.make_async_copy(others, others, chip_sems.at[1, kind]).wait()
        pltpu.make_async_copy(others, others, chip_sems.at[0, kind]).wait()
        result[...] = sum_of([head_in[kind, n] for n in range(n_chip)])
    stores.append(store(0, dq_ref, dq_out))
    stores.append(store(1, dk_ref, dk_out))
    for copy in stores:
        copy.wait()


def finish(pieces, *refs):
    half = len(pieces)
    given, results, held = refs[:half], refs[half : 2 * half], refs[2 * half : 3 * half]
    load_sems, store_sems = refs[3 * half :]
    steps = []
    for ref, out, mid, count in zip(given, results, held, pieces):
        size = ref.shape[0] // count
        for at in range(count):
            cut = pl.ds(at * size, size)
            i = len(steps)
            steps.append(
                (
                    pltpu.make_async_copy(ref.at[cut], mid.at[cut], load_sems.at[i]),
                    pltpu.make_async_copy(mid.at[cut], out.at[cut], store_sems.at[i]),
                )
            )
    for load, _ in steps:
        load.start()
    for load, store in steps:
        load.wait()
        store.start()
    for _, store in steps:
        store.wait()


def shards(queries, keys, values, gates, level_weights, segment, cotangent):
    n_ctx, n_head = lax.axis_size("ctx"), lax.axis_size("head")
    heads, tokens = gates.shape
    num = tokens // STRETCH
    bits = n_ctx.bit_length() - 1
    slab_rows = heads * STRETCH // n_ctx
    held = pltpu.VMEM((n_ctx * bits, slab_rows, STRETCH), F32)
    single = pltpu.VMEM((n_ctx, slab_rows, STRETCH), F32)
    turned = pltpu.VMEM((STRETCH, tokens), F32)
    turned_half = pltpu.VMEM((STRETCH, tokens), BF16)

    def chunks(n):
        return pltpu.VMEM((2, n, STRETCH, STRETCH), F32)

    anywhere = pl.BlockSpec(memory_space=pl.ANY)
    rows_out = tokens // n_head
    weights = level_weights.transpose(1, 0, 2)
    segments = segment.reshape(num, STRETCH)
    inputs = (queries, keys, values, cotangent, gates, weights, segments)
    results = (
        jax.ShapeDtypeStruct((rows_out, STRETCH), F32),
        jax.ShapeDtypeStruct((rows_out, STRETCH), F32),
        jax.ShapeDtypeStruct(values.shape, F32),
        jax.ShapeDtypeStruct(gates.shape, F32),
        jax.ShapeDtypeStruct(weights.shape, F32),
    )
    raw = pl.pallas_call(
        functools.partial(kernel, n_ctx, n_head),
        out_shape=results,
        in_specs=[anywhere] * 7,
        out_specs=(anywhere,) * 5,
        scratch_shapes=[
            *[pltpu.VMEM(x.shape, x.dtype) for x in (*results, *inputs)],
            turned,
            turned,
            turned_half,
            turned_half,
            pltpu.VMEM((heads, STRETCH, tokens), BF16),
            pltpu.VMEM((heads, num, STRETCH, STRETCH), F32),
            single,
            single,
            held,
            held,
            held,
            held,
            single,
            single,
            turned,
            pltpu.VMEM((tokens, STRETCH), F32),
            pltpu.VMEM((heads, tokens, STRETCH), F32),
            pltpu.VMEM((5, heads * num, 1, STRETCH), F32),
            pltpu.VMEM((heads, 1, STRETCH), F32),
            pltpu.VMEM((n_ctx, 1, STRETCH), F32),
            pltpu.VMEM((n_ctx, 1, STRETCH), F32),
            pltpu.VMEM((n_ctx, 1, STRETCH), F32),
            chunks(n_head),
            chunks(n_head // 2),
            chunks(n_head // 2),
            pltpu.SemaphoreType.DMA((14,)),
            pltpu.SemaphoreType.DMA((2, 2, n_head // 2)),
            pltpu.SemaphoreType.DMA((2, 2)),
            pltpu.SemaphoreType.DMA((7,)),
            pltpu.SemaphoreType.DMA((5,)),
        ],
        compiler_params=pltpu.CompilerParams(
            collective_id=0, has_side_effects=True, vmem_limit_bytes=56 * 2**20
        ),
        name="loglinear_backward",
    )(*inputs)
    pieces = (1, 1, 4, 1, 1)
    *outs, weight_grad = pl.pallas_call(
        functools.partial(finish, pieces),
        out_shape=[jax.ShapeDtypeStruct(x.shape, F32) for x in raw],
        in_specs=[anywhere] * len(raw),
        out_specs=[anywhere] * len(raw),
        scratch_shapes=[
            *[pltpu.VMEM(x.shape, F32) for x in raw],
            pltpu.SemaphoreType.DMA((sum(pieces),)),
            pltpu.SemaphoreType.DMA((sum(pieces),)),
        ],
        name="store_results",
    )(*raw)
    return (*outs, weight_grad.transpose(1, 0, 2))


def solution(mesh):
    return jax.shard_map(
        shards,
        mesh=mesh,
        in_specs=(
            P("ctx", None),
            P("ctx", None),
            P("ctx", "head"),
            P("head", "ctx"),
            P("head", None, "ctx"),
            P("ctx"),
            P("ctx", "head"),
        ),
        out_specs=(
            P(("ctx", "head"), None),
            P(("ctx", "head"), None),
            P("ctx", "head"),
            P("head", "ctx"),
            P("head", None, "ctx"),
        ),
        check_vma=False,
    )
```

```python
import functools

import jax
import jax.numpy as jnp
from jax import lax
from jax.experimental import pallas as pl
from jax.experimental.pallas import tpu as pltpu
from jax.sharding import PartitionSpec as P

STRETCH = 128
LOCAL_LEVELS = 3
F32 = jnp.float32
BF16 = jnp.bfloat16


def halves(x):
    high = x.astype(BF16)
    return high, (x - high.astype(F32)).astype(BF16)


def thirds(x):
    high = x.astype(BF16)
    rest = x - high.astype(F32)
    middle = rest.astype(BF16)
    return high, middle, (rest - middle.astype(F32)).astype(BF16)


def dot(a, b):
    return jnp.dot(a, b, preferred_element_type=F32)


def dot_nt(a, b):
    return lax.dot_general(a, b, (((1,), (1,)), ((), ())), preferred_element_type=F32)


def dot_left(x, exact):
    high, low = halves(x)
    return dot(high, exact) + dot(low, exact)


def dot_right(exact, x):
    high, low = halves(x)
    return dot(exact, high) + dot(exact, low)


def sum_of(terms):
    return functools.reduce(jnp.add, terms)


def ones_where(mask):
    return jnp.where(mask, 1.0, 0.0).astype(BF16)


def part(c):
    return slice(c * STRETCH, (c + 1) * STRETCH)


def pop(number, bits):
    return sum_of([(number >> b) & 1 for b in range(bits)])


def kernel(
    n_ctx,
    n_head,
    q_in,
    k_in,
    v_in,
    c_in,
    g_in,
    w_in,
    s_in,
    dq_out,
    dk_out,
    dv_out,
    dg_out,
    dw_out,
    dq_ref,
    dk_ref,
    dv_ref,
    dg_ref,
    dw_ref,
    q_ref,
    k_ref,
    v_ref,
    c_ref,
    g_ref,
    w_ref,
    s_ref,
    qt_ref,
    kt_ref,
    qtb_ref,
    ktb_ref,
    ctb_ref,
    block_ref,
    s_out,
    s_in_buf,
    out1,
    buf1,
    out2,
    buf2,
    t_out,
    t_in,
    dqt_ref,
    dk_acc,
    product_ref,
    row_ref,
    meta_out,
    meta_in,
    flow_out,
    flow_in,
    head_out,
    pair_in,
    head_in,
    sems,
    pair_sems,
    chip_sems,
    in_sems,
    out_sems,
):
    loads = [
        pltpu.make_async_copy(source, target, in_sems.at[i])
        for i, (source, target) in enumerate(
            [
                (g_in, g_ref),
                (s_in, s_ref),
                (k_in, k_ref),
                (v_in, v_ref),
                (q_in, q_ref),
                (c_in, c_ref),
                (w_in, w_ref),
            ]
        )
    ]
    for load in loads:
        load.start()
    heads, tokens = g_ref.shape
    num = tokens // STRETCH
    rows = heads * num
    bits = n_ctx.bit_length() - 1
    slabs = bits
    slab_rows = buf1.shape[1]
    per_head = n_ctx // heads
    me = lax.axis_index("ctx")
    mine = lax.axis_index("head")
    count = pop(me, bits)
    everything = sum(bin(n).count("1") for n in range(n_ctx))

    def partner(k):
        step = (k + 1) // 2
        return lax.rem(jnp.where(lax.rem(k, 2) == 1, me + step, me + n_ctx - step), n_ctx)

    barrier = pltpu.get_barrier_semaphore()

    def greet_ctx(k, _):
        pl.semaphore_signal(barrier, inc=1, device_id={"ctx": lax.rem(me + k, n_ctx)})
        return 0

    def greet_head(k, _):
        pl.semaphore_signal(barrier, inc=1, device_id={"head": lax.rem(mine + k, n_head)})
        return 0

    lax.fori_loop(1, n_ctx, greet_ctx, 0)
    lax.fori_loop(1, n_head, greet_head, 0)

    for load in loads[:2]:
        load.wait()

    gates = jnp.concatenate(
        [g_ref[h : h + 1, part(c)] for h in range(heads) for c in range(num)], axis=0
    )
    seg_one = s_ref[...]
    seg = jnp.concatenate([seg_one] * heads, axis=0)
    row_at = lax.broadcasted_iota(jnp.int32, (STRETCH, STRETCH), 0)
    lane_at = lax.broadcasted_iota(jnp.int32, (STRETCH, STRETCH), 1)
    upto = ones_where(row_at <= lane_at)
    within = sum_of([dot(x, upto) for x in thirds(gates)])
    total = jnp.broadcast_to(within[:, STRETCH - 1 :], within.shape)
    seg_end = jnp.broadcast_to(seg[:, STRETCH - 1 :], seg.shape)
    seg_first = jnp.broadcast_to(seg_one[:, :1], seg_one.shape)[:1]
    ra = lax.broadcasted_iota(jnp.int32, (rows, rows), 0)
    rb = lax.broadcasted_iota(jnp.int32, (rows, rows), 1)
    same_head = (ra // num) == (rb // num)
    earlier = ones_where(same_head & (rb < ra))
    later = ones_where(same_head & (rb > ra))
    before = sum_of([dot(earlier, x) for x in thirds(total)])
    entry = jnp.where(seg == seg_first, jnp.exp(within + before), 0.0)
    key_weight = jnp.where(seg == seg_end, jnp.exp(total - within), 0.0)
    through_exp = jnp.exp(total)

    def end(c):
        return seg_end[c : c + 1]

    def through(h, c):
        r = h * num + c
        return jnp.where(end(c - 1) == end(c), through_exp[r : r + 1], 0.0)

    def local_weight(h, level, c):
        r = h * num + c
        span = 1 << (level - 1)
        base = c // span * span
        shift = before[r : r + 1] - before[h * num + base : h * num + base + 1]
        return jnp.where(
            seg[r : r + 1] == end(base - 1), jnp.exp(within[r : r + 1] + shift), 0.0
        )

    def remote_row(h, k, c):
        picked = jnp.zeros((1, STRETCH), F32)
        for b in range(bits):
            is_it = (((me >> b) & 1) == 1) & (pop(me & ((1 << b) - 1), bits) == k)
            level = LOCAL_LEVELS + 1 + b
            picked = picked + jnp.where(is_it, w_ref[level, h : h + 1, part(c)], 0.0)
        return picked

    def columns(ref, h):
        return ref[:, h * STRETCH : (h + 1) * STRETCH]

    for load in loads[2:4]:
        load.wait()
    kt_ref[...] = k_ref[...].astype(F32).T

    def send_state(h, k, _):
        to = partner(k)

        @pl.when(to // per_head == h)
        def _():
            pltpu.make_async_remote_copy(
                src_ref=meta_out.at[h],
                dst_ref=meta_in.at[me],
                send_sem=sems.at[6],
                recv_sem=sems.at[7],
                device_id={"ctx": to},
            ).start()
            pltpu.make_async_remote_copy(
                src_ref=s_out.at[to],
                dst_ref=s_in_buf.at[me],
                send_sem=sems.at[10],
                recv_sem=sems.at[11],
                device_id={"ctx": to},
            ).start()

        return 0

    for h in range(heads):
        for c in range(num):
            r = h * num + c
            scaled = kt_ref[:, part(c)] * key_weight[r : r + 1]
            block_ref[h, c] = dot_left(scaled, v_ref[part(c), h * STRETCH : (h + 1) * STRETCH])
        state = block_ref[h, 0]
        for c in range(1, num):
            state = through(h, c) * state + block_ref[h, c]
        last = h * num + num - 1
        passes = jnp.where(
            seg_first == end(num - 1), jnp.exp(before[last : last + 1] + total[last : last + 1]), 0.0
        )
        at = lax.broadcasted_iota(jnp.int32, (1, STRETCH), 1)
        meta_out[h] = jnp.where(
            at < 32,
            passes,
            jnp.where(at < 64, seg_first.astype(F32), end(num - 1).astype(F32)),
        )
        for i in range(per_head):
            s_out[h * per_head + i] = state[i * slab_rows : (i + 1) * slab_rows]
        if h == 0:
            pl.semaphore_wait(barrier, n_ctx + n_head - 2)
        lax.fori_loop(1, n_ctx, functools.partial(send_state, h), 0)

    meta_in[me] = meta_out[me // per_head]
    s_in_buf[me] = s_out[me]

    for load in loads[4:]:
        load.wait()
    qt_ref[...] = q_ref[...].astype(F32).T

    for k in range(bits):

        @pl.when(count > k)
        def _(k=k):
            for h in range(heads):
                scaled = jnp.concatenate(
                    [
                        qt_ref[:, part(c)]
                        * (entry[h * num + c : h * num + c + 1] * remote_row(h, k, c))
                        for c in range(num)
                    ],
                    axis=1,
                )
                grad = dot_left(scaled, columns(c_ref, h))
                for i in range(per_head):
                    out1[(h * per_head + i) * slabs + k] = grad[
                        i * slab_rows : (i + 1) * slab_rows
                    ]

    for size in range(1, bits + 1):

        @pl.when(count == size)
        def _(size=size):
            def send(k, _):
                to = partner(k)
                pltpu.make_async_remote_copy(
                    src_ref=out1.at[pl.ds(to * slabs, size)],
                    dst_ref=buf1.at[pl.ds(me * slabs, size)],
                    send_sem=sems.at[0],
                    recv_sem=sems.at[1],
                    device_id={"ctx": to},
                ).start()
                return 0

            lax.fori_loop(1, n_ctx, send, 0)
            for s in range(size):
                buf1[me * slabs + s] = out1[me * slabs + s]

    qtb_ref[...] = qt_ref[...].astype(BF16)
    ktb_ref[...] = kt_ref[...].astype(BF16)
    for h in range(heads):
        ctb_ref[h] = columns(c_ref, h).astype(F32).T.astype(BF16)

    got_state = s_in_buf.at[pl.ds(0, n_ctx - 1)]
    pltpu.make_async_copy(got_state, got_state, sems.at[11]).wait()
    got_meta = meta_in.at[pl.ds(0, n_ctx - 1)]
    pltpu.make_async_copy(got_meta, got_meta, sems.at[7]).wait()
    meta_rows = [
        [jnp.broadcast_to(meta_in[n][:, i : i + 1], (1, STRETCH)) for i in (0, 32, 64)]
        for n in range(n_ctx)
    ]
    enter = [None] + [
        jnp.where(meta_rows[n - 1][2] == meta_rows[n][1], 1.0, 0.0) for n in range(1, n_ctx)
    ]
    link = [jnp.zeros_like(meta_rows[0][0])] + [
        meta_rows[n][0] * enter[n] for n in range(1, n_ctx)
    ]

    def rank(n, b):
        return bin(n & ((1 << b) - 1)).count("1")

    blocks = [s_in_buf[n] for n in range(n_ctx)]
    passing = [link]
    factors = {}
    for b in range(bits):
        thru = passing[b]
        for j in range(1, n_ctx >> b, 2):
            lead = None
            for p in range(j << b, (j + 1) << b):
                lead = jnp.ones((1, STRETCH), F32) if lead is None else lead * link[p - 1]
                factors[b, p] = lead * enter[p]
                out2[p * slabs + rank(p, b)] = factors[b, p] * blocks[j - 1]
        half = len(blocks) // 2
        blocks = [thru[2 * j + 1] * blocks[2 * j] + blocks[2 * j + 1] for j in range(half)]
        passing.append([thru[2 * j] * thru[2 * j + 1] for j in range(half)])

    def send_buckets(k, _):
        to = partner(k)
        size_there = pop(to, bits)
        for size in range(1, bits + 1):

            @pl.when(size_there == size)
            def _(size=size):
                pltpu.make_async_remote_copy(
                    src_ref=out2.at[pl.ds(to * slabs, size)],
                    dst_ref=buf2.at[pl.ds(me * slabs, size)],
                    send_sem=sems.at[2],
                    recv_sem=sems.at[3],
                    device_id={"ctx": to},
                ).start()

        return 0

    lax.fori_loop(1, n_ctx, send_buckets, 0)
    for size in range(1, bits + 1):

        @pl.when(count == size)
        def _(size=size):
            for s in range(size):
                buf2[me * slabs + s] = out2[me * slabs + s]

    ones = jnp.ones((8, STRETCH), BF16)
    query_terms = [None] * rows
    for c in range(num):
        seg_row = seg_one[c : c + 1]
        seg_col = jnp.broadcast_to(seg_row.astype(F32), (STRETCH, STRETCH)).T
        allowed = (row_at <= lane_at) & (seg_col == seg_row.astype(F32))
        scores = dot(k_ref[part(c), :], qtb_ref[:, part(c)])
        dk_sum = None
        dq_sum = None
        for h in range(heads):
            r = h * num + c
            cols = slice(h * STRETCH, (h + 1) * STRETCH)
            w_row = within[r : r + 1]
            w_col = jnp.broadcast_to(w_row, (STRETCH, STRETCH)).T
            decay = jnp.where(allowed, jnp.exp(jnp.minimum(w_row - w_col, 0.0)), 0.0)
            pairs = dot(v_ref[part(c), cols], ctb_ref[h, :, part(c)])
            mixed = decay * scores
            weight = w_ref[0, h : h + 1, part(c)]
            d_weight = jnp.sum(mixed * pairs, axis=0, keepdims=True)
            dw_ref[0, h : h + 1, part(c)] = d_weight
            query_terms[r] = weight * d_weight
            dv_ref[part(c), cols] = dot_left(mixed * weight, c_ref[part(c), cols])
            d_scores = decay * pairs * weight
            dk_one = dot_left(d_scores, q_ref[part(c), :])
            dq_one = dot_right(ktb_ref[:, part(c)], d_scores)
            product_ref[h, part(c), :] = k_ref[part(c), :].astype(F32) * dk_one
            dk_sum = dk_one if dk_sum is None else dk_sum + dk_one
            dq_sum = dq_one if dq_sum is None else dq_sum + dq_one
        dk_acc[part(c), :] = dk_sum
        dqt_ref[:, part(c)] = dq_sum

    for size in range(bits + 1):

        @pl.when(count == size)
        def _(size=size):
            got = buf1.at[pl.ds(0, everything - size)]
            pltpu.make_async_copy(got, got, sems.at[1]).wait()

    block_grads = [[None] * (n_ctx >> b) for b in range(bits)]
    for b in range(bits):
        for j in range(1, n_ctx >> b, 2):
            block_grads[b][j - 1] = sum_of(
                [
                    factors[b, p] * buf1[p * slabs + rank(p, b)]
                    for p in range(j << b, (j + 1) << b)
                ]
            )
    down = [jnp.zeros((slab_rows, STRETCH), F32)]
    for b in reversed(range(bits)):
        next_down = []
        for j, top in enumerate(down):
            next_down += [block_grads[b][2 * j] + passing[b][2 * j + 1] * top, top]
        down = next_down
    for n in range(n_ctx):
        t_out[n] = down[n]

    def send_grads(k, _):
        to = partner(k)
        pltpu.make_async_remote_copy(
            src_ref=t_out.at[to],
            dst_ref=t_in.at[me],
            send_sem=sems.at[12],
            recv_sem=sems.at[13],
            device_id={"ctx": to},
        ).start()
        return 0

    lax.fori_loop(1, n_ctx, send_grads, 0)
    t_in[me] = t_out[me]

    after = jnp.zeros((slab_rows, STRETCH), F32)
    for n in reversed(range(n_ctx)):
        flow_out[n] = jnp.sum(after, axis=0, keepdims=True)
        after = after - s_in_buf[n] * t_out[n]
        for slot in range(n * slabs, n * slabs + bin(n).count("1")):
            after = after + out2[slot] * buf1[slot]

    def send_flows(k, _):
        to = partner(k)
        pltpu.make_async_remote_copy(
            src_ref=flow_out.at[to],
            dst_ref=flow_in.at[me],
            send_sem=sems.at[8],
            recv_sem=sems.at[9],
            device_id={"ctx": to},
        ).start()
        return 0

    lax.fori_loop(1, n_ctx, send_flows, 0)
    flow_in[me] = flow_out[me]

    state_grads = []
    for h in range(heads):
        cols = slice(h * STRETCH, (h + 1) * STRETCH)
        lower = [block_ref[h, c] for c in range(num)]
        thru = [None] + [through(h, c) for c in range(1, num)]
        thru[0] = jnp.zeros_like(thru[1])
        per_level = []
        thrus = []
        for level in range(1, LOCAL_LEVELS + 1):
            span = 1 << (level - 1)
            grads = [None] * len(lower)
            for j in range(1, len(lower), 2):
                lanes = slice(j * span * STRETCH, (j + 1) * span * STRETCH)
                high, low = halves(lower[j - 1])
                reach = ctb_ref[h, :, lanes]
                got = dot(high, reach) + dot(low, reach)
                scaled = []
                for c in range(j * span, (j + 1) * span):
                    r = h * num + c
                    here = slice((c - j * span) * STRETCH, (c - j * span + 1) * STRETCH)
                    decay = local_weight(h, level, c)
                    q_part = qt_ref[:, part(c)]
                    d_weight = decay * jnp.sum(q_part * got[:, here], axis=0, keepdims=True)
                    weight = w_ref[level, h : h + 1, part(c)]
                    dw_ref[level, h : h + 1, part(c)] = d_weight
                    query_terms[r] = query_terms[r] + weight * d_weight
                    both = weight * decay
                    dqt_ref[:, part(c)] += both * got[:, here]
                    scaled.append(q_part * both)
                scaled = jnp.concatenate(scaled, axis=1) if span > 1 else scaled[0]
                grads[j - 1] = dot_left(scaled, c_ref[lanes, cols])
            for j in range(0, len(lower), 2):
                for c in range(j * span, (j + 1) * span):
                    dw_ref[level, h : h + 1, part(c)] = jnp.zeros((1, STRETCH), F32)
            per_level.append(grads)
            thrus.append(thru)
            lower, thru = (
                [thru[j + 1] * lower[j] + lower[j + 1] for j in range(0, len(lower), 2)],
                [thru[j] * thru[j + 1] for j in range(0, len(lower), 2)],
            )
        down = [None]
        for level in reversed(range(LOCAL_LEVELS)):
            next_down = []
            for j, top in enumerate(down):
                low = per_level[level][2 * j]
                next_down += [low if top is None else low + thrus[level][2 * j + 1] * top, top]
            down = next_down
        for c in range(num - 1):
            block_ref[h, c] = down[c]
        block_ref[h, num - 1] = jnp.zeros((STRETCH, STRETCH), F32)
        state_grads.append(None)

    for size in range(1, bits + 1):

        @pl.when(count == size)
        def _(size=size):
            got = buf2.at[pl.ds(0, (n_ctx - 1) * size)]
            pltpu.make_async_copy(got, got, sems.at[3]).wait()

    def gathered(ref, stride, s, h):
        return jnp.concatenate(
            [ref[(h * per_head + i) * stride + s] for i in range(per_head)], axis=0
        )

    dw_ref[LOCAL_LEVELS + 1 :] = jnp.zeros(
        (dw_ref.shape[0] - LOCAL_LEVELS - 1, heads, tokens), F32
    )
    for k in range(bits):

        @pl.when(count > k)
        def _(k=k):
            for h in range(heads):
                high, low = halves(gathered(buf2, slabs, k, h))
                for c in range(num):
                    reach = ctb_ref[h, :, part(c)]
                    got = dot(high, reach) + dot(low, reach)
                    decay = entry[h * num + c : h * num + c + 1]
                    d_weight = decay * jnp.sum(qt_ref[:, part(c)] * got, axis=0, keepdims=True)
                    dqt_ref[:, part(c)] += (decay * remote_row(h, k, c)) * got
                    for b in range(bits):
                        is_it = (((me >> b) & 1) == 1) & (pop(me & ((1 << b) - 1), bits) == k)
                        level = LOCAL_LEVELS + 1 + b
                        dw_ref[level, h : h + 1, part(c)] += jnp.where(is_it, d_weight, 0.0)

    n_chip = n_head // 2
    core, chip = lax.rem(mine, 2), mine // 2
    sibling = chip * 2 + 1 - core

    def send_pair(kind, x, source):
        pltpu.make_async_remote_copy(
            src_ref=source,
            dst_ref=pair_in.at[kind, x],
            send_sem=pair_sems.at[0, kind, x],
            recv_sem=pair_sems.at[1, kind, x],
            device_id={"head": sibling},
        ).start()

    def join(kind, x):
        arrived = pair_in.at[kind, x]
        pltpu.make_async_copy(arrived, arrived, pair_sems.at[1, kind, x]).wait()
        pair_in[kind, x] = pair_in[kind, x] + head_out[kind, 2 * x + core]

    def send_chip(kind, x):
        join(kind, x)
        pltpu.make_async_remote_copy(
            src_ref=pair_in.at[kind, x],
            dst_ref=head_in.at[kind, chip],
            send_sem=chip_sems.at[0, kind],
            recv_sem=chip_sems.at[1, kind],
            device_id={"head": x * 2 + core},
        ).start()

    def send_if_siblings(kind, c):
        @pl.when(core != c % 2)
        def _():
            send_pair(kind, c // 2, head_out.at[kind, c])

    for c in range(num):
        head_out[0, c] = dqt_ref[:, part(c)].T
        send_if_siblings(0, c)
    for k in range(1, n_chip):
        send_chip(0, lax.rem(chip + k, n_chip))
    join(0, chip)
    head_in[0, chip] = pair_in[0, chip]

    for h in range(heads):
        reach = jnp.ones((1, STRETCH), F32)
        for c in reversed(range(num)):
            r = h * num + c
            row_ref[0, r] = within[r : r + 1]
            row_ref[1, r] = total[r : r + 1]
            row_ref[2, r] = end(c).astype(F32)
            row_ref[3, r] = seg_one[c : c + 1].astype(F32)
            row_ref[4, r] = reach
            if c:
                reach = reach * through(h, c)

    got_grads = t_in.at[pl.ds(0, n_ctx - 1)]
    pltpu.make_async_copy(got_grads, got_grads, sems.at[13]).wait()
    tops = [gathered(t_in, 1, 0, h) for h in range(heads)]

    def finish_keys(c):
        here = pl.ds(pl.multiple_of(c * STRETCH, STRETCH), STRETCH)
        seg_col = jnp.broadcast_to(row_ref[3, c], (STRETCH, STRETCH)).T
        keys_here = k_ref[here, :]
        dk_sum = dk_acc[here, :]
        for h in range(heads):
            cols = slice(h * STRETCH, (h + 1) * STRETCH)
            r = h * num + c
            w_col = jnp.broadcast_to(row_ref[0, r], (STRETCH, STRETCH)).T
            weight = jnp.where(
                seg_col == row_ref[2, r], jnp.exp(row_ref[1, r] - w_col), 0.0
            )
            high, low = halves(block_ref[h, c] + row_ref[4, r] * tops[h])
            values_here = v_ref[here, cols]
            dv_ref[here, cols] += weight * (dot(keys_here, high) + dot(keys_here, low))
            dk_one = weight * (dot_nt(values_here, high) + dot_nt(values_here, low))
            dk_sum = dk_sum + dk_one
            product_ref[h, here, :] += keys_here.astype(F32) * dk_one
        head_out[1, c] = dk_sum

    chip_order = [lax.rem(chip + k, n_chip) for k in range(1, n_chip + 1)]
    for k, x in enumerate(chip_order):
        finish_keys(2 * x + 1 - core)
        send_pair(1, x, head_out.at[1, 2 * x + 1 - core])
        finish_keys(2 * x + core)
        if k:
            send_chip(1, chip_order[k - 1])
    join(1, chip)
    head_in[1, chip] = pair_in[1, chip]

    def store(i, source, target):
        copy = pltpu.make_async_copy(source, target, out_sems.at[i])
        copy.start()
        return copy

    stores = [store(2, dv_ref, dv_out), store(4, dw_ref, dw_out)]

    got_flow = flow_in.at[pl.ds(0, n_ctx - 1)]
    pltpu.make_async_copy(got_flow, got_flow, sems.at[9]).wait()
    from_here = ones_where(row_at >= lane_at)
    terms = []
    for h in range(heads):
        for c in range(num):
            r = h * num + c
            sums = sum_of([dot_nt(ones, x) for x in thirds(product_ref[h, part(c), :])])
            term = query_terms[r] - sums[:1]
            for level in range(LOCAL_LEVELS + 1, LOCAL_LEVELS + 1 + bits):
                term = term + w_ref[level, h : h + 1, part(c)] * dw_ref[
                    level, h : h + 1, part(c)
                ]
            terms.append(term)
    terms = jnp.concatenate(terms, axis=0)
    suffix = sum_of([dot(x, from_here) for x in thirds(terms)])
    sums = jnp.broadcast_to(suffix[:, :1], suffix.shape)
    suffix = suffix + sum_of([dot(later, x) for x in thirds(sums)])
    for h in range(heads):
        beyond = sum_of([flow_in[h * per_head + i] for i in range(per_head)])
        beyond = jnp.sum(beyond, axis=1, keepdims=True)
        for c in range(num):
            r = h * num + c
            dg_ref[h : h + 1, part(c)] = suffix[r : r + 1] + beyond
    stores.append(store(3, dg_ref, dg_out))

    for size in range(bits + 1):

        @pl.when(count == size)
        def _(size=size):
            if size:
                sent = out1.at[pl.ds(0, (n_ctx - 1) * size)]
                pltpu.make_async_copy(sent, sent, sems.at[0]).wait()
            sent = out2.at[pl.ds(0, everything - size)]
            pltpu.make_async_copy(sent, sent, sems.at[2]).wait()

    sent = meta_in.at[pl.ds(0, n_ctx - 1)]
    pltpu.make_async_copy(sent, sent, sems.at[6]).wait()
    pltpu.make_async_copy(sent, sent, sems.at[8]).wait()
    sent = s_out.at[pl.ds(0, n_ctx - 1)]
    pltpu.make_async_copy(sent, sent, sems.at[10]).wait()
    pltpu.make_async_copy(sent, sent, sems.at[12]).wait()
    others = head_in.at[0, pl.ds(0, n_chip - 1)]
    for kind, result in enumerate((dq_ref, dk_ref)):
        for x in range(n_chip):
            sent = pair_in.at[kind, x]
            pltpu.make_async_copy(sent, sent, pair_sems.at[0, kind, x]).wait()
        pltpu.make_async_copy(others, others, chip_sems.at[1, kind]).wait()
        pltpu.make_async_copy(others, others, chip_sems.at[0, kind]).wait()
        result[...] = sum_of([head_in[kind, n] for n in range(n_chip)])
    stores.append(store(0, dq_ref, dq_out))
    stores.append(store(1, dk_ref, dk_out))
    for copy in stores:
        copy.wait()


def finish(pieces, *refs):
    half = len(pieces)
    given, results, held = refs[:half], refs[half : 2 * half], refs[2 * half : 3 * half]
    load_sems, store_sems = refs[3 * half :]
    steps = []
    for ref, out, mid, count in zip(given, results, held, pieces):
        size = ref.shape[0] // count
        for at in range(count):
            cut = pl.ds(at * size, size)
            i = len(steps)
            steps.append(
                (
                    pltpu.make_async_copy(ref.at[cut], mid.at[cut], load_sems.at[i]),
                    pltpu.make_async_copy(mid.at[cut], out.at[cut], store_sems.at[i]),
                )
            )
    for load, _ in steps:
        load.start()
    for load, store in steps:
        load.wait()
        store.start()
    for _, store in steps:
        store.wait()


def shards(queries, keys, values, gates, level_weights, segment, cotangent):
    n_ctx, n_head = lax.axis_size("ctx"), lax.axis_size("head")
    heads, tokens = gates.shape
    num = tokens // STRETCH
    bits = n_ctx.bit_length() - 1
    slab_rows = heads * STRETCH // n_ctx
    held = pltpu.VMEM((n_ctx * bits, slab_rows, STRETCH), F32)
    single = pltpu.VMEM((n_ctx, slab_rows, STRETCH), F32)
    turned = pltpu.VMEM((STRETCH, tokens), F32)
    turned_half = pltpu.VMEM((STRETCH, tokens), BF16)

    def chunks(n):
        return pltpu.VMEM((2, n, STRETCH, STRETCH), F32)

    anywhere = pl.BlockSpec(memory_space=pl.ANY)
    rows_out = tokens // n_head
    weights = level_weights.transpose(1, 0, 2)
    segments = segment.reshape(num, STRETCH)
    inputs = (queries, keys, values, cotangent, gates, weights, segments)
    results = (
        jax.ShapeDtypeStruct((rows_out, STRETCH), F32),
        jax.ShapeDtypeStruct((rows_out, STRETCH), F32),
        jax.ShapeDtypeStruct(values.shape, F32),
        jax.ShapeDtypeStruct(gates.shape, F32),
        jax.ShapeDtypeStruct(weights.shape, F32),
    )
    raw = pl.pallas_call(
        functools.partial(kernel, n_ctx, n_head),
        out_shape=results,
        in_specs=[anywhere] * 7,
        out_specs=(anywhere,) * 5,
        scratch_shapes=[
            *[pltpu.VMEM(x.shape, x.dtype) for x in (*results, *inputs)],
            turned,
            turned,
            turned_half,
            turned_half,
            pltpu.VMEM((heads, STRETCH, tokens), BF16),
            pltpu.VMEM((heads, num, STRETCH, STRETCH), F32),
            single,
            single,
            held,
            held,
            held,
            held,
            single,
            single,
            turned,
            pltpu.VMEM((tokens, STRETCH), F32),
            pltpu.VMEM((heads, tokens, STRETCH), F32),
            pltpu.VMEM((5, heads * num, 1, STRETCH), F32),
            pltpu.VMEM((heads, 1, STRETCH), F32),
            pltpu.VMEM((n_ctx, 1, STRETCH), F32),
            pltpu.VMEM((n_ctx, 1, STRETCH), F32),
            pltpu.VMEM((n_ctx, 1, STRETCH), F32),
            chunks(n_head),
            chunks(n_head // 2),
            chunks(n_head // 2),
            pltpu.SemaphoreType.DMA((14,)),
            pltpu.SemaphoreType.DMA((2, 2, n_head // 2)),
            pltpu.SemaphoreType.DMA((2, 2)),
            pltpu.SemaphoreType.DMA((7,)),
            pltpu.SemaphoreType.DMA((5,)),
        ],
        compiler_params=pltpu.CompilerParams(
            collective_id=0, has_side_effects=True, vmem_limit_bytes=56 * 2**20
        ),
        name="loglinear_backward",
    )(*inputs)
    pieces = (1, 1, 4, 1, 1)
    *outs, weight_grad = pl.pallas_call(
        functools.partial(finish, pieces),
        out_shape=[jax.ShapeDtypeStruct(x.shape, F32) for x in raw],
        in_specs=[anywhere] * len(raw),
        out_specs=[anywhere] * len(raw),
        scratch_shapes=[
            *[pltpu.VMEM(x.shape, F32) for x in raw],
            pltpu.SemaphoreType.DMA((sum(pieces),)),
            pltpu.SemaphoreType.DMA((sum(pieces),)),
        ],
        name="store_results",
    )(*raw)
    return (*outs, weight_grad.transpose(1, 0, 2))


def solution(mesh):
    return jax.shard_map(
        shards,
        mesh=mesh,
        in_specs=(
            P("ctx", None),
            P("ctx", None),
            P("ctx", "head"),
            P("head", "ctx"),
            P("head", None, "ctx"),
            P("ctx"),
            P("ctx", "head"),
        ),
        out_specs=(
            P(("ctx", "head"), None),
            P(("ctx", "head"), None),
            P("ctx", "head"),
            P("head", "ctx"),
            P("head", None, "ctx"),
        ),
        check_vma=False,
    )
```
